32 devices in a mesh: groups: 2 (over y), tiles: 4 (over z), rows: 2 (over x), comp: 2 (over core).
Axes of the slice: x: 2, y: 2, z: 4, core: 2. Of those that a mesh axis runs over, the one named last changes fastest.
Arguments:
- atmos_grid_state: bfloat16 [256, 256, 256], P(('groups', 'comp'), 'tiles', 'rows'), parts along dimension 0, may hold values from -6 to 6
- sea_field_values: bfloat16 [192, 256, 256], P(('groups', 'comp'), 'tiles', 'rows'), parts along dimension 0, may hold values from -6 to 6
- atmos_depthwise_kernel: float32 [128, 3, 3], P('comp'), may hold values from -2 to 2
- air_from_sea_linear_map: bfloat16 [128, 96], replicated, may hold values from -0.625 to 0.625
- air_standardize_scaling_factor: float32 [128], replicated, may hold values from 0.1 to 1.9
- air_standardize_additive_shift: float32 [128], replicated, may hold values from -3 to 3
- air_widening_linear_map: bfloat16 [256, 128], replicated, may hold values from -0.5 to 0.5
- air_widening_additive_shift: float32 [256], replicated, may hold values from -3 to 3
- air_narrowing_linear_map: bfloat16 [128, 256], replicated, may hold values from -0.375 to 0.375
- ocean_depthwise_kernel: float32 [96, 3, 3], P('comp'), may hold values from -2 to 2
- ocean_coupling_matrix: bfloat16 [96, 128], replicated, may hold values from -0.5 to 0.5
- ocean_layer_norm_gain: float32 [96], replicated, may hold values from 0.1 to 1.9
- ocean_layer_norm_bias: float32 [96], replicated, may hold values from -3 to 3
- ocean_expand_matrix: bfloat16 [192, 96], replicated, may hold values from -0.625 to 0.625
- ocean_expand_offset_bias: float32 [192], replicated, may hold values from -3 to 3
- ocean_project_matrix: bfloat16 [96, 192], replicated, may hold values from -0.4375 to 0.4375
- heat_flux_source_cell: int32 [512, 128], P(('tiles', 'rows')), may hold values from 0 to 8191
- heat_flux_target_cell: int32 [512, 128], P(('tiles', 'rows')), may hold values from 0 to 8191
- heat_flux_margin_weight: float32 [512, 128], P(('tiles', 'rows')), may hold values from 0.25 to 1
- heat_flux_heading: int32 [512, 1], P(('tiles', 'rows')), may hold values from 0 to 8, as said below
- seawarmth_sender_location: int32 [512, 128], P(('tiles', 'rows')), may hold values from 0 to 8191
- seawarmth_receiver_location: int32 [512, 128], P(('tiles', 'rows')), may hold values from 0 to 8191
- seawarmth_overlay_fraction: float32 [512, 128], P(('tiles', 'rows')), may hold values from 0.25 to 1
- seawarmth_direction: int32 [512, 1], P(('tiles', 'rows')), may hold values from 0 to 8, as said below
Outputs:
- atm_next: bfloat16 [256, 256, 256], P(('groups', 'comp'), 'tiles', 'rows'), parts along dimension 0
- ocn_next: bfloat16 [192, 256, 256], P(('groups', 'comp'), 'tiles', 'rows'), parts along dimension 0
The draws below stay inside these ranges and needn't reach their ends.
There are 2 independent parts, one for each index of `groups`. The reference program is written for one: setup_inputs(seed, part) draws one part's arguments, and reference() takes and returns one part's arrays. A program takes and returns all parts, laid end to end along the dimension named above; an argument that names none is the same for every part. Nothing has to cross between parts.
Inputs may be any that keep to these rules, and one draw needn't show every extreme that they name: `heat_flux_heading`: tiles of the first band use no heading below 3; tiles of the last band use neither 6 nor 8. Exactly 16 blocks of every source tile have heading 4, and no heading has more than 16 blocks of one source tile. `seawarmth_direction`: tiles of the first band use no heading below 3; tiles of the last band use neither 6 nor 8. Exactly 16 blocks of every source tile have heading 4, and no heading has more than 16 blocks of one source tile.
All inputs are finite; a program needn't handle non-finite values.
Results may differ from the reference program's by a relative error of at most 0.0058.
Values may be sent and summed in bfloat16 or wider, within the bound.
A program may use at most 128 MiB of HBM per device.

```python
import jax
import jax.numpy as jnp
from jax import lax

CA = 128
CO = 96
AIR_LATITUDE_SPAN = 64
AIR_LONGITUDE_SPAN = 128
SEA_LATITUDE_SPAN = 64
SEA_LONGITUDE_SPAN = 128
BLOCK_ROWS = 128
KBA = 64
SEA_TO_AIR_GROUPS = 64
GRID_TILES = 8
SBA = 16
SBO = 16
N_TILES = 4
N_ROWS = 2


def deal_headings(key, blocks, most):
    peers = N_TILES * N_ROWS
    keys = jax.random.split(key, peers)
    ranks = jax.vmap(lambda one_key: jax.random.permutation(one_key, blocks))(keys).astype(jnp.int32)
    band = jnp.arange(peers, dtype=jnp.int32) // N_ROWS
    headings = jnp.arange(9, dtype=jnp.int32)
    lifts = headings // 3
    sides = headings % 3
    below = (band[:, None] == 0) & (lifts[None, :] == 0)
    corner = (band[:, None] == N_TILES - 1) & (lifts[None, :] == 2) & (sides[None, :] != 1)
    allowed = (headings[None, :] != 4) & jnp.logical_not(below) & jnp.logical_not(corner)
    scores = jnp.where(allowed, 0, 16).astype(jnp.int32) + headings[None, :]
    order = jnp.argsort(scores, axis=1).astype(jnp.int32)
    usable = jnp.sum(allowed.astype(jnp.int32), axis=1)
    spare = jnp.maximum(ranks - most, 0) % usable[:, None]
    picked = jnp.take_along_axis(order, spare, axis=1)
    result = jnp.where(ranks < most, 4, picked)
    return result.reshape(peers * blocks, 1).astype(jnp.int32)


def draw_heat_flux_heading(key, part):
    key = jax.random.fold_in(key, 11)
    return deal_headings(key, KBA, SBA)


def draw_seawarmth_direction(key, part):
    key = jax.random.fold_in(key, 23)
    return deal_headings(key, SEA_TO_AIR_GROUPS, SBO)


def place_ends(array, stream_key, least, largest):
    longest = array.shape.index(max(array.shape))
    spots = []
    for shift in (0, 1):
        where = [jax.random.randint(jax.random.fold_in(stream_key, axis), (), 0, length) for axis, length in enumerate(array.shape)]
        where[longest] = (where[longest] + shift) % array.shape[longest]
        spots.append(tuple(where))
    return array.at[spots[0]].set(least).at[spots[1]].set(largest)


def level_of(own_key, shape, pieces, smallest, largest):
    def one(axis_at, blocks):
        draws = jax.random.uniform(jax.random.fold_in(jax.random.fold_in(own_key, 6), axis_at), (blocks,), jnp.float32, smallest / len(pieces), largest / len(pieces))
        return jnp.repeat(jnp.exp(draws), shape[axis_at] // blocks).reshape((-1,) + (1,) * (len(shape) - axis_at - 1))

    factor_of = one(*pieces[0])
    for cut in pieces[1:]:
        factor_of = factor_of * one(*cut)
    return factor_of


def gaussian(rng, shape, scale, reach, pieces=(), kind=jnp.bfloat16):
    values = jax.random.normal(rng, shape, jnp.float32) * scale
    if len(pieces) > 0:
        values = level_of(rng, shape, pieces, -0.22, 0.18) * values
    return jnp.clip(values, min=-reach, max=reach).astype(kind)


def setup_inputs(seed: int = 0, part: int = 0) -> dict:
    key_of = jax.random.split(jax.random.key(seed), 25)
    part_keys = jax.random.split(jax.random.fold_in(key_of[24], part), 25)
    atmos_grid_state = gaussian(part_keys[0], (CA, AIR_LATITUDE_SPAN * N_TILES, AIR_LONGITUDE_SPAN * N_ROWS), 1.0, 6.0, ((0, 2), (1, 4), (2, 2)))
    sea_field_values = gaussian(part_keys[1], (CO, SEA_LATITUDE_SPAN * N_TILES, SEA_LONGITUDE_SPAN * N_ROWS), 1.0, 6.0, ((0, 2), (1, 4), (2, 2)))
    atmos_depthwise_kernel = gaussian(key_of[2], (CA, 3, 3), 9 ** -0.5, 2.0, ((0, 2),), jnp.float32)
    air_from_sea_linear_map = gaussian(key_of[3], (CA, CO), CO ** -0.5, 0.625)
    air_standardize_scaling_factor = jnp.clip(1.0 + 0.18 * jax.random.normal(key_of[4], (CA,), jnp.float32), 0.1, 1.9)
    air_standardize_additive_shift = gaussian(key_of[5], (CA,), 0.5, 3.0, (), jnp.float32)
    air_widening_linear_map = gaussian(key_of[6], (2 * CA, CA), CA ** -0.5, 0.5)
    air_widening_additive_shift = gaussian(key_of[7], (2 * CA,), 0.5, 3.0, (), jnp.float32)
    air_narrowing_linear_map = gaussian(key_of[8], (CA, 2 * CA), (2 * CA) ** -0.5, 0.375)
    ocean_depthwise_kernel = gaussian(key_of[9], (CO, 3, 3), 9 ** -0.5, 2.0, ((0, 2),), jnp.float32)
    ocean_coupling_matrix = gaussian(key_of[10], (CO, CA), CA ** -0.5, 0.5)
    ocean_layer_norm_gain = jnp.clip(1.0 + 0.18 * jax.random.normal(key_of[11], (CO,), jnp.float32), 0.1, 1.9)
    ocean_layer_norm_bias = gaussian(key_of[12], (CO,), 0.5, 3.0, (), jnp.float32)
    ocean_expand_matrix = gaussian(key_of[13], (2 * CO, CO), CO ** -0.5, 0.625)
    ocean_expand_offset_bias = gaussian(key_of[14], (2 * CO,), 0.5, 3.0, (), jnp.float32)
    ocean_project_matrix = gaussian(key_of[15], (CO, 2 * CO), (2 * CO) ** -0.5, 0.4375)
    heat_flux_source_cell = place_ends(jax.random.randint(key_of[16], (GRID_TILES * KBA, BLOCK_ROWS), 0, AIR_LATITUDE_SPAN * AIR_LONGITUDE_SPAN), jax.random.fold_in(key_of[16], 1), 0, (AIR_LATITUDE_SPAN * AIR_LONGITUDE_SPAN) - 1).astype(jnp.int32)
    heat_flux_target_cell = place_ends(jax.random.randint(key_of[17], (GRID_TILES * KBA, BLOCK_ROWS), 0, SEA_LATITUDE_SPAN * SEA_LONGITUDE_SPAN), jax.random.fold_in(key_of[17], 1), 0, (SEA_LATITUDE_SPAN * SEA_LONGITUDE_SPAN) - 1).astype(jnp.int32)
    heat_flux_margin_weight = jnp.clip(0.25 + 0.75 * jax.random.uniform(key_of[18], (GRID_TILES * KBA, BLOCK_ROWS), jnp.float32) ** level_of(key_of[18], (GRID_TILES * KBA, BLOCK_ROWS), ((0, 8),), -0.2, 0.2), 0.25, 1.0)
    heat_flux_heading = draw_heat_flux_heading(jax.random.fold_in(key_of[24], 71), part)
    seawarmth_sender_location = place_ends(jax.random.randint(key_of[20], (GRID_TILES * SEA_TO_AIR_GROUPS, BLOCK_ROWS), 0, SEA_LATITUDE_SPAN * SEA_LONGITUDE_SPAN), jax.random.fold_in(key_of[20], 1), 0, (SEA_LATITUDE_SPAN * SEA_LONGITUDE_SPAN) - 1).astype(jnp.int32)
    seawarmth_receiver_location = place_ends(jax.random.randint(key_of[21], (GRID_TILES * SEA_TO_AIR_GROUPS, BLOCK_ROWS), 0, AIR_LATITUDE_SPAN * AIR_LONGITUDE_SPAN), jax.random.fold_in(key_of[21], 1), 0, (AIR_LATITUDE_SPAN * AIR_LONGITUDE_SPAN) - 1).astype(jnp.int32)
    seawarmth_overlay_fraction = jnp.clip(0.25 + 0.75 * jax.random.uniform(key_of[22], (GRID_TILES * SEA_TO_AIR_GROUPS, BLOCK_ROWS), jnp.float32) ** level_of(key_of[22], (GRID_TILES * SEA_TO_AIR_GROUPS, BLOCK_ROWS), ((0, 8),), -0.2, 0.2), 0.25, 1.0)
    seawarmth_direction = draw_seawarmth_direction(jax.random.fold_in(key_of[24], 71), part)
    return {"atmos_grid_state": atmos_grid_state, "sea_field_values": sea_field_values, "atmos_depthwise_kernel": atmos_depthwise_kernel, "air_from_sea_linear_map": air_from_sea_linear_map, "air_standardize_scaling_factor": air_standardize_scaling_factor, "air_standardize_additive_shift": air_standardize_additive_shift, "air_widening_linear_map": air_widening_linear_map, "air_widening_additive_shift": air_widening_additive_shift, "air_narrowing_linear_map": air_narrowing_linear_map, "ocean_depthwise_kernel": ocean_depthwise_kernel, "ocean_coupling_matrix": ocean_coupling_matrix, "ocean_layer_norm_gain": ocean_layer_norm_gain, "ocean_layer_norm_bias": ocean_layer_norm_bias, "ocean_expand_matrix": ocean_expand_matrix, "ocean_expand_offset_bias": ocean_expand_offset_bias, "ocean_project_matrix": ocean_project_matrix, "heat_flux_source_cell": heat_flux_source_cell, "heat_flux_target_cell": heat_flux_target_cell, "heat_flux_margin_weight": heat_flux_margin_weight, "heat_flux_heading": heat_flux_heading, "seawarmth_sender_location": seawarmth_sender_location, "seawarmth_receiver_location": seawarmth_receiver_location, "seawarmth_overlay_fraction": seawarmth_overlay_fraction, "seawarmth_direction": seawarmth_direction}


def conservative_regridding(field, sources, targets, weights, headings, blocks, src_h, src_w, dst_h, dst_w, dst_rows, dst_cols):
    chans = field.shape[0]
    src_cols = field.shape[2]
    flat = field.reshape(chans, -1)

    def one_device(device, total):
        device = jnp.asarray(device).astype(jnp.int32)
        start = (device * blocks).astype(jnp.int32)
        src = lax.dynamic_slice_in_dim(sources, start, blocks, 0)
        dst = lax.dynamic_slice_in_dim(targets, start, blocks, 0)
        wgt = lax.dynamic_slice_in_dim(weights, start, blocks, 0)
        head = lax.dynamic_slice_in_dim(headings, start, blocks, 0)
        band = device // N_ROWS
        strip = device % N_ROWS
        src_flat = (band * src_h + src // src_w) * src_cols + strip * src_w + src % src_w
        lift = head // 3 - 1
        sideways = (strip + head % 3 - 1 + N_ROWS) % N_ROWS
        across = (band == N_TILES - 1) & (lift == 1)
        dest_band = jnp.where(across, band, band + lift)
        dest_strip = jnp.where(across, N_ROWS - 1 - sideways, sideways)
        dst_flat = (dest_band * dst_h + dst // dst_w) * dst_cols + dest_strip * dst_w + dst % dst_w
        picked = jnp.take(flat, src_flat.reshape(-1).astype(jnp.int32), axis=1).astype(jnp.float32)
        values = (picked * wgt.reshape(-1)[None, :]).astype(jnp.bfloat16)
        values = lax.optimization_barrier(values).astype(jnp.float32)
        return total.at[:, dst_flat.reshape(-1).astype(jnp.int32)].add(values)
    total = lax.fori_loop(0, N_TILES * N_ROWS, one_device, jnp.zeros((chans, dst_rows * dst_cols), jnp.float32))
    return total.astype(jnp.bfloat16).reshape(chans, dst_rows, dst_cols)

def convolve(field, kernel, folded_blocks):
    wide = jnp.concatenate([field[:, :, -1:], field, field[:, :, :1]], axis=2)
    south = jnp.zeros_like(wide[:, :1, :])
    if folded_blocks:
        north = wide[:, -1:, ::-1]
    else:
        north = south
    padded = jnp.concatenate([south, wide, north], axis=1).astype(jnp.float32)
    height, width = (field.shape[1], field.shape[2])
    total = jnp.zeros(field.shape, jnp.float32)
    for row in range(3):
        for col in range(3):
            total = total + kernel[:, row, col][:, None, None] * padded[:, row:row + height, col:col + width]
    return total.astype(jnp.bfloat16)

def feature_combination(conv, coupled, coupling, gain, shift, expand, expand_bias, project, band_rows):
    chans, height, width = conv.shape

    def one_band(band):
        start = (band * band_rows).astype(jnp.int32)
        piece = lax.dynamic_slice_in_dim(conv, start, band_rows, 1).astype(jnp.float32)
        near = lax.dynamic_slice_in_dim(coupled, start, band_rows, 1).astype(jnp.float32)
        mixed = piece + jnp.einsum('cq,qyx->cyx', coupling.astype(jnp.float32), near)
        mean = lax.optimization_barrier(jnp.mean(mixed, axis=0, keepdims=True))
        centred = mixed - mean
        var = lax.optimization_barrier(jnp.mean(centred * centred, axis=0, keepdims=True))
        normed = (centred * lax.rsqrt(var + 1e-06) * gain[:, None, None] + shift[:, None, None]).astype(jnp.bfloat16)
        hidden = jnp.einsum('hc,cyx->hyx', expand.astype(jnp.float32), normed.astype(jnp.float32)) + expand_bias[:, None, None]
        hidden = jax.nn.gelu(hidden, approximate=True).astype(jnp.bfloat16)
        update = jnp.einsum('ch,hyx->cyx', project.astype(jnp.float32), hidden.astype(jnp.float32))
        return update.astype(jnp.bfloat16)
    parts = lax.map(one_band, jnp.arange(height // band_rows, dtype=jnp.int32))
    return jnp.transpose(parts, (1, 0, 2, 3)).reshape(chans, height, width)

def reference(atmos_grid_state, sea_field_values, atmos_depthwise_kernel, air_from_sea_linear_map, air_standardize_scaling_factor, air_standardize_additive_shift, air_widening_linear_map, air_widening_additive_shift, air_narrowing_linear_map, ocean_depthwise_kernel, ocean_coupling_matrix, ocean_layer_norm_gain, ocean_layer_norm_bias, ocean_expand_matrix, ocean_expand_offset_bias, ocean_project_matrix, heat_flux_source_cell, heat_flux_target_cell, heat_flux_margin_weight, heat_flux_heading, seawarmth_sender_location, seawarmth_receiver_location, seawarmth_overlay_fraction, seawarmth_direction):
    flux = conservative_regridding(atmos_grid_state, heat_flux_source_cell, heat_flux_target_cell, heat_flux_margin_weight, heat_flux_heading, KBA, AIR_LATITUDE_SPAN, AIR_LONGITUDE_SPAN, SEA_LATITUDE_SPAN, SEA_LONGITUDE_SPAN, SEA_LATITUDE_SPAN * N_TILES, SEA_LONGITUDE_SPAN * N_ROWS)
    seawater_warmth = conservative_regridding(sea_field_values, seawarmth_sender_location, seawarmth_receiver_location, seawarmth_overlay_fraction, seawarmth_direction, SEA_TO_AIR_GROUPS, SEA_LATITUDE_SPAN, SEA_LONGITUDE_SPAN, AIR_LATITUDE_SPAN, AIR_LONGITUDE_SPAN, AIR_LATITUDE_SPAN * N_TILES, AIR_LONGITUDE_SPAN * N_ROWS)
    air_residual_unit = convolve(atmos_grid_state, atmos_depthwise_kernel, False)
    ocn_conv = convolve(sea_field_values, ocean_depthwise_kernel, True)
    air_field_advance = feature_combination(air_residual_unit, seawater_warmth, air_from_sea_linear_map, air_standardize_scaling_factor, air_standardize_additive_shift, air_widening_linear_map, air_widening_additive_shift, air_narrowing_linear_map, AIR_LATITUDE_SPAN)
    ocn_update = feature_combination(ocn_conv, flux, ocean_coupling_matrix, ocean_layer_norm_gain, ocean_layer_norm_bias, ocean_expand_matrix, ocean_expand_offset_bias, ocean_project_matrix, SEA_LATITUDE_SPAN)
    atm_next = (atmos_grid_state.astype(jnp.float32) + air_field_advance.astype(jnp.float32)).astype(jnp.bfloat16)
    ocn_next = (sea_field_values.astype(jnp.float32) + ocn_update.astype(jnp.float32)).astype(jnp.bfloat16)
    return (atm_next, ocn_next)
```

```python
import functools

import jax
import jax.numpy as jnp
from jax import lax
from jax.experimental import pallas as pl
from jax.experimental.pallas import tpu as pltpu
from jax.sharding import PartitionSpec as P

SLOTS = 16
META = 112
LANES = 256
GROUP = 8
VMEM_LIMIT = 56 * 1024 * 1024
BF = jnp.bfloat16
F32 = jnp.float32
MESH = pl.DeviceIdType.MESH


def pack_kernel(bounds, slots_ref, state_ref, halo_ref, pos_ref, high_ref, weight_ref, meta_ref, out_ref):
    flat_slots = SLOTS + 1
    pairs = state_ref.shape[0] // 2

    def clear(i, _):
        out_ref[i // SLOTS, lax.rem(i, SLOTS), META:, :] = jnp.full((16, 128), -1, BF)
        return 0

    lax.fori_loop(0, 9 * SLOTS, clear, 0)
    for k in range(9):
        out_ref[k, flat_slots - 1] = halo_ref[k]
    column = lax.broadcasted_iota(jnp.int32, (LANES, LANES), 0).astype(F32).astype(BF)
    row16 = lax.broadcasted_iota(jnp.int32, (16, 128), 0)

    def step(j, _):
        for f, (low, high) in enumerate(bounds):
            chans = high - low
            hit = jnp.broadcast_to(pos_ref[f, j], (LANES, LANES)).astype(BF) == column
            onehot = jnp.where(hit, jnp.ones((), BF), jnp.zeros((), BF))
            wanted = jnp.broadcast_to(high_ref[f, j], (chans, LANES))
            total = jnp.zeros((chans, LANES), F32)
            for first in range(0, pairs, GROUP):
                lhs = jnp.concatenate(
                    [
                        jnp.concatenate(
                            [state_ref[2 * q, low:high, :], state_ref[2 * q + 1, low:high, :]], axis=1
                        )
                        for q in range(first, first + GROUP)
                    ],
                    axis=0,
                )
                part = jnp.dot(lhs, onehot, preferred_element_type=F32)
                for q in range(GROUP):
                    total = jnp.where(
                        wanted == float(first + q), part[q * chans : (q + 1) * chans], total
                    )
            values = (total * weight_ref[f, j]).astype(BF)
            for half in range(2):
                block = 2 * j + half
                slot = slots_ref[f, block]
                k, s = slot // SLOTS, lax.rem(slot, SLOTS)
                out_ref[k, s, low:high, :] = values[:, half * 128 : (half + 1) * 128]
                old = out_ref[k, s, META:, :].astype(F32)
                for item in range(2):
                    place = jnp.broadcast_to(meta_ref[f, item, block], (16, 128))
                    old = jnp.where(row16 == 2 * f + item, place, old)
                out_ref[k, s, META:, :] = old.astype(BF)
        return 0

    lax.fori_loop(0, slots_ref.shape[1] // 2, step, 0)


def send_kernel(n_tiles, n_rows, packed_ref, got_ref, send_sem, recv_sem, local_sem):
    band = lax.axis_index("tiles")
    strip = lax.axis_index("rows")
    last = n_tiles - 1
    barrier = pltpu.get_barrier_semaphore()
    routes = []
    for k in (0, 2, 6, 8, 3, 5, 1, 7):
        lift, side = k // 3 - 1, k % 3 - 1
        to = {"tiles": band + lift, "rows": lax.rem(strip + side + n_rows, n_rows)}
        sends = (band + lift >= 0) & (band + lift <= last)
        receives = (band - lift >= 0) & (band - lift <= last)
        routes.append((k, k, to, sends, receives))
    routes.append((7, 9, {"rows": n_rows - 1 - strip}, band == last, band == last))

    peers = []
    for lift in (-1, 0, 1):
        for side in (0, 1) if n_rows == 2 else (-1, 0, 1):
            if (lift, side) != (0, 0):
                to = {"tiles": band + lift, "rows": lax.rem(strip + side + n_rows, n_rows)}
                peers.append((to, (band + lift >= 0) & (band + lift <= last)))
    if n_rows > 2:
        mirror = n_rows - 1 - strip
        beside = (mirror == lax.rem(strip + 1, n_rows)) | (mirror == lax.rem(strip + n_rows - 1, n_rows))
        peers.append(({"rows": mirror}, (band == last) & jnp.logical_not(beside)))
    for to, there in peers:

        @pl.when(there)
        def _():
            pl.semaphore_signal(barrier, inc=1, device_id=to, device_id_type=MESH)

    pl.semaphore_wait(barrier, sum(there.astype(jnp.int32) for _, there in peers))

    def copy(i):
        src, dst, to, _, _ = routes[i]
        return pltpu.make_async_remote_copy(
            src_ref=packed_ref.at[src],
            dst_ref=got_ref.at[dst],
            send_sem=send_sem.at[i],
            recv_sem=recv_sem.at[i],
            device_id=to,
            device_id_type=MESH,
        )

    for i, route in enumerate(routes):

        @pl.when(route[3])
        def _():
            copy(i).start()

    own = pltpu.make_async_copy(packed_ref.at[4], got_ref.at[4], local_sem)
    own.start()
    own.wait()
    for i, route in enumerate(routes):

        @pl.when(route[3])
        def _():
            copy(i).wait_send()

        @pl.when(route[4])
        def _():
            copy(i).wait_recv()


def land_kernel(
    bounds, outs, order_ref, count_ref, got_ref, state_ref, edge_ref, cols_ref, taps_ref,
    out_ref, acc_ref,
):
    height = state_ref.shape[0]
    chans = state_ref.shape[1]
    row_of = lax.broadcasted_iota(jnp.int32, (256, 128), 0)
    lane_of = lax.broadcasted_iota(jnp.int32, (256, 128), 1)
    lane = lax.broadcasted_iota(jnp.int32, (chans, 128), 1)
    cols = cols_ref[...]

    def taps(i, row):
        pick = ((row_of == i) & (lane_of == 0)) | ((row_of == i + 128) & (lane_of == 127))
        ends = jnp.dot(cols, pick.astype(F32).astype(BF), preferred_element_type=F32)
        row = row.astype(F32)
        left = jnp.where(lane == 0, ends, pltpu.roll(row, 1, 1))
        right = jnp.where(lane == 127, ends, pltpu.roll(row, 127, 1))
        return [
            taps_ref[3 * r] * left + taps_ref[3 * r + 1] * row + taps_ref[3 * r + 2] * right
            for r in range(3)
        ]

    def put(y, value):
        value = value.astype(BF)
        out_ref[y, 0:chans, :] = value

    h0 = taps(0, edge_ref[0])
    h1 = taps(1, state_ref[0])

    def conv(i, carry):
        older, newer = carry
        h = taps(i, state_ref[i - 1])
        put(i - 2, older + h[2])
        return newer + h[1], h[0]

    older, newer = lax.fori_loop(2, height + 1, conv, (h0[0] + h1[1], h1[0]))
    h = taps(height + 1, edge_ref[1])
    put(height - 1, older + h[2])

    column = lax.broadcasted_iota(jnp.int32, (LANES, GROUP * 128), 0).astype(F32).astype(BF)
    pairs = height // 2
    for f, (low, high) in enumerate(bounds):
        width = high - low
        count = count_ref[f]
        acc_ref[...] = jnp.zeros_like(acc_ref)

        def step(j, _):
            vals, high_of, low_of = [], [], []
            for b in range(GROUP):
                at = order_ref[f, j * GROUP + b]
                vals.append(got_ref[at, low:high, :])
                meta = got_ref[at, META:, :].astype(F32)
                live = j * GROUP + b < count
                high_of.append(jnp.where(live, meta[2 * f : 2 * f + 1], -1.0))
                low_of.append(jnp.where(live, meta[2 * f + 1 : 2 * f + 2], -1.0))
            vals = jnp.concatenate(vals, axis=1)
            high_of = jnp.concatenate(high_of, axis=1)
            low_of = jnp.concatenate(low_of, axis=1)
            hit = jnp.broadcast_to(low_of, (LANES, GROUP * 128)).astype(BF) == column
            onehot = jnp.where(hit, jnp.ones((), BF), jnp.zeros((), BF))
            wanted = jnp.broadcast_to(high_of, (width, GROUP * 128)).astype(BF)
            for first in range(0, pairs, 8):
                lhs = jnp.concatenate(
                    [
                        jnp.where(wanted == jnp.asarray(first + q, BF), vals, jnp.zeros((), BF))
                        for q in range(8)
                    ],
                    axis=0,
                )
                acc_ref[first * width : (first + 8) * width, :] += lax.dot_general(
                    lhs, onehot, (((1,), (1,)), ((), ())), preferred_element_type=F32
                )
            return 0

        lax.fori_loop(0, (count + GROUP - 1) // GROUP, step, 0)
        begin = outs[f]
        for q in range(pairs):
            piece = acc_ref[q * width : (q + 1) * width, :].astype(BF)
            out_ref[2 * q, begin : begin + width, :] = piece[:, :128]
            out_ref[2 * q + 1, begin : begin + width, :] = piece[:, 128:]


def mix_kernel(ca, co, in_ref, coup_a, vec_a, exp_a, eb_a, proj_a, coup_o, vec_o, exp_o, eb_o, proj_o, out_ref):
    rows = in_ref.shape[0]
    half_a, half_o = ca // 2, co // 2
    part = half_a + half_o
    whole = 2 * part

    def lanes(low, size):
        return jnp.concatenate(
            [
                jnp.concatenate(
                    [in_ref[y, low : low + size, :], in_ref[y, whole + low : whole + low + size, :]], axis=0
                )
                for y in range(rows)
            ],
            axis=1,
        )

    def unit(conv, coupled, coup, vec, expand, bias, project):
        mixed = conv.astype(F32) + jnp.dot(coup[...], coupled, preferred_element_type=F32)
        mean = jnp.mean(mixed, axis=0, keepdims=True)
        centred = mixed - mean
        var = jnp.mean(centred * centred, axis=0, keepdims=True)
        normed = (centred * lax.rsqrt(var + 1e-6) * vec[:, 0:1] + vec[:, 1:2]).astype(BF)
        hidden = jnp.dot(expand[...], normed, preferred_element_type=F32) + bias[...]
        hidden = jax.nn.gelu(hidden, approximate=True).astype(BF)
        return jnp.dot(project[...], hidden, preferred_element_type=F32).astype(BF)

    air = unit(lanes(0, half_a), lanes(part, half_o), coup_a, vec_a, exp_a, eb_a, proj_a)
    sea = unit(lanes(half_a, half_o), lanes(part + half_o, half_a), coup_o, vec_o, exp_o, eb_o, proj_o)
    for y in range(rows):
        at = slice(y * 128, (y + 1) * 128)
        for side in range(2):
            base = side * part
            out_ref[y, base : base + half_a, :] = air[side * half_a : (side + 1) * half_a, at]
            out_ref[y, base + half_a : base + part, :] = sea[side * half_o : (side + 1) * half_o, at]


def slots_of(heading):
    lanes = heading[:, 0]
    n = lanes.shape[0]
    i = jnp.arange(n, dtype=jnp.int32)
    before = (lanes[:, None] == lanes[None, :]) & (i[None, :] < i[:, None])
    return lanes * SLOTS + jnp.sum(before.astype(jnp.int32), axis=1)


def compact(valid):
    n = valid.shape[0]
    i = jnp.arange(n, dtype=jnp.int32)
    where = jnp.sum((valid[None, :] & (i[None, :] < i[:, None])).astype(jnp.int32), axis=1)
    at = (i // SLOTS) * (SLOTS + 1) + i % SLOTS
    chosen = valid[None, :] & (where[None, :] == i[:, None])
    return jnp.sum(jnp.where(chosen, at[None, :], 0), axis=1), jnp.sum(valid.astype(jnp.int32))


def local(
    atm, sea, atm_kernel, atm_coupling, atm_gain, atm_shift, atm_expand, atm_expand_bias, atm_project,
    sea_kernel, sea_coupling, sea_gain, sea_shift, sea_expand, sea_expand_bias, sea_project,
    flux_source, flux_target, flux_weight, flux_heading, sst_source, sst_target, sst_weight, sst_heading,
):
    n_tiles, n_rows = lax.axis_size("tiles"), lax.axis_size("rows")
    band = lax.axis_index("tiles")
    last = n_tiles - 1
    half_a, half_o = atm.shape[0], sea.shape[0]
    part = half_a + half_o
    height, width = atm.shape[1], atm.shape[2]
    blocks = flux_source.shape[0]
    bounds = ((0, half_a), (half_a, part))
    params = functools.partial(pltpu.CompilerParams, vmem_limit_bytes=VMEM_LIMIT)
    vmem = pl.BlockSpec(memory_space=pltpu.VMEM)
    smem = pl.BlockSpec(memory_space=pltpu.SMEM)

    state = jnp.transpose(jnp.concatenate([atm, sea], axis=0), (1, 0, 2))

    def fit(a):
        return jnp.pad(a, ((0, 128 - a.shape[0]), (0, 128 - a.shape[1])))

    south_row, north_row = fit(state[0]), fit(state[height - 1])
    west_col, east_col = fit(state[:, :, 0].T), fit(state[:, :, width - 1].T)
    halo = jnp.stack(
        [south_row, south_row, south_row, west_col, west_col, east_col, north_row, north_row, north_row]
    )
    slots = jnp.stack([slots_of(flux_heading), slots_of(sst_heading)])
    source = jnp.stack([flux_source, sst_source])
    target = jnp.stack([flux_target, sst_target])
    weight = jnp.stack([flux_weight, sst_weight])

    def paired(a):
        return a.astype(F32).reshape(2, blocks // 2, 1, 2 * 128)

    meta = jnp.stack([target // LANES, target % LANES], axis=1).astype(F32)[:, :, :, None, :]
    packed = pl.pallas_call(
        functools.partial(pack_kernel, bounds),
        out_shape=jax.ShapeDtypeStruct((9, SLOTS + 1, 128, 128), BF),
        in_specs=[smem] + [vmem] * 6,
        out_specs=vmem,
        compiler_params=params(),
        name="pack",
    )(slots, state, halo, paired(source % LANES), paired(source // LANES), paired(weight), meta)

    got = pl.pallas_call(
        functools.partial(send_kernel, n_tiles, n_rows),
        out_shape=jax.ShapeDtypeStruct((10, SLOTS + 1, 128, 128), BF),
        in_specs=[pl.BlockSpec(memory_space=pl.ANY)],
        out_specs=pl.BlockSpec(memory_space=pl.ANY),
        scratch_shapes=[
            pltpu.SemaphoreType.DMA((9,)),
            pltpu.SemaphoreType.DMA((9,)),
            pltpu.SemaphoreType.DMA,
        ],
        compiler_params=params(collective_id=0, has_side_effects=True),
        name="send",
    )(packed)

    edge = got[:, SLOTS]
    first_band, last_band = band == 0, band == last
    is_air = (jnp.arange(part) < half_a)[:, None]
    south = jnp.where(first_band, 0, edge[7, :part])
    south_w = jnp.where(first_band, 0, edge[8, :part, 127:128])
    south_e = jnp.where(first_band, 0, edge[6, :part, 0:1])

    def across(side):
        perm = [(s, n_rows - 1 - (s + side) % n_rows) for s in range(n_rows)]
        row = state[height - 1]
        if all(a == b for a, b in perm):
            return row
        return lax.ppermute(row, "rows", perm)

    fold = edge[9, :part, ::-1]
    north = jnp.where(last_band, jnp.where(is_air, 0, fold), edge[1, :part])
    north_w = jnp.where(last_band, jnp.where(is_air, 0, across(-1)[:, 0:1]), edge[2, :part, 127:128])
    north_e = jnp.where(last_band, jnp.where(is_air, 0, across(1)[:, 127:128]), edge[0, :part, 0:1])
    zeros = jnp.zeros((part, 128 - height - 2), BF)
    cols = jnp.concatenate(
        [south_w, edge[5, :part, :height], north_w, zeros, south_e, edge[3, :part, :height], north_e, zeros],
        axis=1,
    )
    edges = jnp.stack([south, north])
    taps = jnp.concatenate([atm_kernel, sea_kernel], axis=0).reshape(part, 9).T[:, :, None]
    taps = jnp.broadcast_to(taps, (9, part, 128))

    k = jnp.arange(10)
    usable = jnp.where(k < 3, ~last_band, jnp.where(k < 6, True, jnp.where(k < 9, ~first_band, last_band)))
    listed = got[:, :SLOTS, META : META + 4, 0]
    orders, counts = [], []
    for f in range(2):
        order, count = compact(((listed[:, :, 2 * f] >= 0) & usable[:, None]).reshape(-1))
        orders.append(order)
        counts.append(count)
    mixed_in = pl.pallas_call(
        functools.partial(land_kernel, bounds, (part + half_o, part)),
        out_shape=jax.ShapeDtypeStruct((height, 2 * part, 128), BF),
        in_specs=[smem, smem] + [vmem] * 5,
        out_specs=vmem,
        scratch_shapes=[pltpu.VMEM((height // 2 * half_a, LANES), F32)],
        compiler_params=params(),
        name="land",
    )(
        jnp.stack(orders), jnp.stack(counts), got.reshape(10 * (SLOTS + 1), 128, 128), state, edges, cols, taps
    )

    full = lax.all_to_all(mixed_in, "comp", split_axis=0, concat_axis=1, tiled=True)
    ca, co = 2 * half_a, 2 * half_o
    rows = 4

    def whole(a):
        return pl.BlockSpec(a.shape, lambda i: (0,) * a.ndim)

    weights = [
        atm_coupling, jnp.stack([atm_gain, atm_shift], axis=1), atm_expand, atm_expand_bias[:, None], atm_project,
        sea_coupling, jnp.stack([sea_gain, sea_shift], axis=1), sea_expand, sea_expand_bias[:, None], sea_project,
    ]
    update = pl.pallas_call(
        functools.partial(mix_kernel, ca, co),
        grid=(height // 2 // rows,),
        out_shape=jax.ShapeDtypeStruct((height // 2, 2 * part, 128), BF),
        in_specs=[pl.BlockSpec((rows, 4 * part, 128), lambda i: (i, 0, 0))] + [whole(a) for a in weights],
        out_specs=pl.BlockSpec((rows, 2 * part, 128), lambda i: (i, 0, 0)),
        compiler_params=params(),
        name="mix",
    )(full, *weights)
    update = lax.all_to_all(update, "comp", split_axis=1, concat_axis=0, tiled=True)
    total = jnp.transpose((state.astype(F32) + update.astype(F32)).astype(BF), (1, 0, 2))
    return total[:half_a], total[half_a:]


def solution(mesh):
    grid = P(("groups", "comp"), "tiles", "rows")
    lists = P(("tiles", "rows"), None)
    taps = P("comp", None, None)
    placed = (grid, grid, taps) + (P(),) * 6 + (taps,) + (P(),) * 6 + (lists,) * 8
    return jax.shard_map(local, mesh=mesh, in_specs=placed, out_specs=(grid, grid), check_vma=False)
```

```python
import functools

import jax
import jax.numpy as jnp
from jax import lax
from jax.experimental import pallas as pl
from jax.experimental.pallas import tpu as pltpu
from jax.sharding import PartitionSpec as P

SLOTS = 16
META = 112
LANES = 256
GROUP = 8
VMEM_LIMIT = 56 * 1024 * 1024
BF = jnp.bfloat16
F32 = jnp.float32
MESH = pl.DeviceIdType.MESH


def pack_kernel(bounds, slots_ref, atm_ref, sea_ref, pos_ref, high_ref, weight_ref, meta_ref, out_ref, state_ref):
    height = state_ref.shape[0]
    chans_all = state_ref.shape[1]
    pairs = height // 2
    for field, (low, high) in zip((atm_ref, sea_ref), bounds):
        for y in range(0, height, 16):
            state_ref[y : y + 16, low:high, :] = jnp.swapaxes(field[:, y : y + 16, :], 0, 1)

    def clear(i, _):
        out_ref[i // SLOTS, lax.rem(i, SLOTS), META:, :] = jnp.full((16, 128), -1, BF)
        return 0

    lax.fori_loop(0, 9 * SLOTS, clear, 0)

    row_at = lax.broadcasted_iota(jnp.int32, (128, LANES), 0)
    lane_at = lax.broadcasted_iota(jnp.int32, (128, LANES), 1)

    def column_of(y, total):
        pick = ((row_at == 0) & (lane_at == y)) | ((row_at == 127) & (lane_at == y + 128))
        return total + jnp.dot(state_ref[y], pick.astype(F32).astype(BF), preferred_element_type=F32)

    columns = lax.fori_loop(0, height, column_of, jnp.zeros((chans_all, LANES), F32)).astype(BF)
    for k in range(9):
        if k // 3 == 0:
            out_ref[k, SLOTS, :chans_all, :] = state_ref[0]
        elif k // 3 == 2:
            out_ref[k, SLOTS, :chans_all, :] = state_ref[height - 1]
        elif k == 3:
            out_ref[k, SLOTS, :chans_all, :] = columns[:, :128]
        elif k == 5:
            out_ref[k, SLOTS, :chans_all, :] = columns[:, 128:]

    column = lax.broadcasted_iota(jnp.int32, (LANES, LANES), 0).astype(F32).astype(BF)
    row16 = lax.broadcasted_iota(jnp.int32, (16, 128), 0)

    def step(j, _):
        for f, (low, high) in enumerate(bounds):
            chans = high - low
            hit = jnp.broadcast_to(pos_ref[f, j], (LANES, LANES)).astype(BF) == column
            onehot = jnp.where(hit, jnp.ones((), BF), jnp.zeros((), BF))
            wanted = jnp.broadcast_to(high_ref[f, j], (chans, LANES))
            total = jnp.zeros((chans, LANES), F32)
            for first in range(0, pairs, GROUP):
                lhs = jnp.concatenate(
                    [
                        jnp.concatenate(
                            [state_ref[2 * q, low:high, :], state_ref[2 * q + 1, low:high, :]], axis=1
                        )
                        for q in range(first, first + GROUP)
                    ],
                    axis=0,
                )
                part = jnp.dot(lhs, onehot, preferred_element_type=F32)
                for q in range(GROUP):
                    total = jnp.where(
                        wanted == float(first + q), part[q * chans : (q + 1) * chans], total
                    )
            values = (total * weight_ref[f, j]).astype(BF)
            for half in range(2):
                block = 2 * j + half
                slot = slots_ref[f, block]
                k, s = slot // SLOTS, lax.rem(slot, SLOTS)
                out_ref[k, s, low:high, :] = values[:, half * 128 : (half + 1) * 128]
                old = out_ref[k, s, META:, :].astype(F32)
                for item in range(2):
                    place = jnp.broadcast_to(meta_ref[f, item, block], (16, 128))
                    old = jnp.where(row16 == 2 * f + item, place, old)
                out_ref[k, s, META:, :] = old.astype(BF)
        return 0

    lax.fori_loop(0, slots_ref.shape[1] // 2, step, 0)


def send_kernel(n_tiles, n_rows, packed_ref, got_ref, send_sem, recv_sem, local_sem):
    band = lax.axis_index("tiles")
    strip = lax.axis_index("rows")
    last = n_tiles - 1
    barrier = pltpu.get_barrier_semaphore()
    routes = []
    for k in (0, 2, 6, 8, 3, 5, 1, 7):
        lift, side = k // 3 - 1, k % 3 - 1
        to = {"tiles": band + lift, "rows": lax.rem(strip + side + n_rows, n_rows)}
        sends = (band + lift >= 0) & (band + lift <= last)
        receives = (band - lift >= 0) & (band - lift <= last)
        routes.append((k, k, to, sends, receives))
    routes.append((7, 9, {"rows": n_rows - 1 - strip}, band == last, band == last))

    peers = []
    for lift in (-1, 0, 1):
        for side in (0, 1) if n_rows == 2 else (-1, 0, 1):
            if (lift, side) != (0, 0):
                to = {"tiles": band + lift, "rows": lax.rem(strip + side + n_rows, n_rows)}
                peers.append((to, (band + lift >= 0) & (band + lift <= last)))
    if n_rows > 2:
        mirror = n_rows - 1 - strip
        beside = (mirror == lax.rem(strip + 1, n_rows)) | (mirror == lax.rem(strip + n_rows - 1, n_rows))
        peers.append(({"rows": mirror}, (band == last) & jnp.logical_not(beside)))
    for to, there in peers:

        @pl.when(there)
        def _():
            pl.semaphore_signal(barrier, inc=1, device_id=to, device_id_type=MESH)

    pl.semaphore_wait(barrier, sum(there.astype(jnp.int32) for _, there in peers))

    def copy(i):
        src, dst, to, _, _ = routes[i]
        return pltpu.make_async_remote_copy(
            src_ref=packed_ref.at[src],
            dst_ref=got_ref.at[dst],
            send_sem=send_sem.at[i],
            recv_sem=recv_sem.at[i],
            device_id=to,
            device_id_type=MESH,
        )

    for i, route in enumerate(routes):

        @pl.when(route[3])
        def _():
            copy(i).start()

    own = pltpu.make_async_copy(packed_ref.at[4], got_ref.at[4], local_sem)
    own.start()
    own.wait()
    for i, route in enumerate(routes):

        @pl.when(route[3])
        def _():
            copy(i).wait_send()

        @pl.when(route[4])
        def _():
            copy(i).wait_recv()


def land_kernel(bounds, outs, flags_ref, got_ref, state_ref, across_ref, taps_ref, out_ref, acc_ref, order_ref):
    height = state_ref.shape[0]
    chans = state_ref.shape[1]
    stride = SLOTS + 1
    first_band, last_band = flags_ref[0] == 1, flags_ref[1] == 1
    row_of = lax.broadcasted_iota(jnp.int32, (256, 128), 0)
    lane_of = lax.broadcasted_iota(jnp.int32, (256, 128), 1)
    lane = lax.broadcasted_iota(jnp.int32, (chans, 128), 1)
    is_air = lax.broadcasted_iota(jnp.int32, (chans, 128), 0) < bounds[0][1]

    def edge(k):
        return got_ref[k * stride + SLOTS, :chans, :]

    cols = jnp.concatenate([edge(5), edge(3)], axis=1)
    wide = lax.broadcasted_iota(jnp.int32, (chans, 256), 1) % 128
    cols = jnp.where(wide < height, cols.astype(F32), 0.0).astype(BF)

    def spread(row, left, right):
        return [
            taps_ref[3 * r] * left + taps_ref[3 * r + 1] * row + taps_ref[3 * r + 2] * right
            for r in range(3)
        ]

    def taps(i, row):
        y = i - 1
        pick = ((row_of == y) & (lane_of == 0)) | ((row_of == y + 128) & (lane_of == 127))
        ends = jnp.dot(cols, pick.astype(F32).astype(BF), preferred_element_type=F32)
        row = row.astype(F32)
        left = jnp.where(lane == 0, ends, pltpu.roll(row, 1, 1))
        right = jnp.where(lane == 127, ends, pltpu.roll(row, 127, 1))
        return spread(row, left, right)

    def beyond(row, west, east):
        left = jnp.where(lane == 0, west, pltpu.roll(row, 1, 1))
        right = jnp.where(lane == 127, east, pltpu.roll(row, 127, 1))
        return row, left, right

    def row_from(middle, west, east):
        return beyond(
            edge(middle).astype(F32),
            pltpu.roll(edge(west).astype(F32), 1, 1),
            pltpu.roll(edge(east).astype(F32), 127, 1),
        )

    south = [jnp.where(first_band, 0.0, part) for part in row_from(7, 8, 6)]
    flip_row = lax.broadcasted_iota(jnp.int32, (128, 128), 0)
    flip_lane = lax.broadcasted_iota(jnp.int32, (128, 128), 1)
    flip = (flip_row + flip_lane == 127).astype(F32).astype(BF)
    fold = jnp.where(last_band, edge(9).astype(F32), 0.0).astype(BF)
    fold = jnp.dot(fold, flip, preferred_element_type=F32)
    folded = beyond(fold, across_ref[0].astype(F32), across_ref[1].astype(F32))
    north = [
        jnp.where(last_band, jnp.where(is_air, 0.0, over), part)
        for over, part in zip(folded, row_from(1, 2, 0))
    ]

    def put(y, value):
        value = value.astype(BF)
        out_ref[y, 0:chans, :] = value

    h0 = spread(*south)
    h1 = taps(1, state_ref[0])

    def conv(i, carry):
        older, newer = carry
        h = taps(i, state_ref[i - 1])
        put(i - 2, older + h[2])
        return newer + h[1], h[0]

    older, newer = lax.fori_loop(2, height + 1, conv, (h0[0] + h1[1], h1[0]))
    h = spread(*north)
    put(height - 1, older + h[2])

    column = lax.broadcasted_iota(jnp.int32, (LANES, GROUP * 128), 0).astype(F32).astype(BF)
    pairs = height // 2
    place_row = lax.broadcasted_iota(jnp.int32, (16, 128), 0)
    place_lane = lax.broadcasted_iota(jnp.int32, (16, 128), 1)
    counts = [jnp.int32(0), jnp.int32(0)]
    for k in range(10):
        places = got_ref[k * stride : k * stride + SLOTS, META:, :].astype(F32)
        filled = jnp.sum((places >= 0).astype(F32), axis=0)
        usable = True if 3 <= k < 6 else jnp.logical_not(last_band) if k < 3 else jnp.logical_not(first_band) if k < 9 else last_band
        for f in range(2):
            there = (place_row == 2 * f) & (place_lane == 0)
            count = jnp.sum(jnp.where(there, filled, 0.0)).astype(jnp.int32)
            count = jnp.where(usable, count, 0)
            base = counts[f]

            def note(i, _):
                order_ref[f, base + i] = k * stride + i
                return 0

            lax.fori_loop(0, count, note, 0)
            counts[f] = base + count
    for f, (low, high) in enumerate(bounds):
        width = high - low
        count = counts[f]
        acc_ref[...] = jnp.zeros_like(acc_ref)

        def step(j, _):
            vals, high_of, low_of = [], [], []
            for b in range(GROUP):
                at = order_ref[f, jnp.minimum(j * GROUP + b, count - 1)]
                vals.append(got_ref[at, low:high, :])
                meta = got_ref[at, META:, :].astype(F32)
                live = j * GROUP + b < count
                high_of.append(jnp.where(live, meta[2 * f : 2 * f + 1], -1.0))
                low_of.append(jnp.where(live, meta[2 * f + 1 : 2 * f + 2], -1.0))
            vals = jnp.concatenate(vals, axis=1)
            high_of = jnp.concatenate(high_of, axis=1)
            low_of = jnp.concatenate(low_of, axis=1)
            hit = jnp.broadcast_to(low_of, (LANES, GROUP * 128)).astype(BF) == column
            onehot = jnp.where(hit, jnp.ones((), BF), jnp.zeros((), BF))
            wanted = jnp.broadcast_to(high_of, (width, GROUP * 128)).astype(BF)
            for first in range(0, pairs, 8):
                lhs = jnp.concatenate(
                    [
                        jnp.where(wanted == jnp.asarray(first + q, BF), vals, jnp.zeros((), BF))
                        for q in range(8)
                    ],
                    axis=0,
                )
                acc_ref[first * width : (first + 8) * width, :] += lax.dot_general(
                    lhs, onehot, (((1,), (1,)), ((), ())), preferred_element_type=F32
                )
            return 0

        lax.fori_loop(0, (count + GROUP - 1) // GROUP, step, 0)
        begin = outs[f]
        for q in range(pairs):
            piece = acc_ref[q * width : (q + 1) * width, :].astype(BF)
            out_ref[2 * q, begin : begin + width, :] = piece[:, :128]
            out_ref[2 * q + 1, begin : begin + width, :] = piece[:, 128:]


def mix_kernel(ca, co, in_ref, coup_a, vec_a, exp_a, eb_a, proj_a, coup_o, vec_o, exp_o, eb_o, proj_o, out_ref):
    rows = in_ref.shape[1]
    half_a, half_o = ca // 2, co // 2
    part = half_a + half_o

    def lanes(low, size):
        return jnp.concatenate(
            [
                jnp.concatenate([in_ref[0, y, low : low + size, :], in_ref[1, y, low : low + size, :]], axis=0)
                for y in range(rows)
            ],
            axis=1,
        )

    def unit(conv, coupled, coup, vec, expand, bias, project):
        mixed = conv.astype(F32) + jnp.dot(coup[...], coupled, preferred_element_type=F32)
        mean = jnp.mean(mixed, axis=0, keepdims=True)
        centred = mixed - mean
        var = jnp.mean(centred * centred, axis=0, keepdims=True)
        normed = (centred * lax.rsqrt(var + 1e-6) * vec[:, 0:1] + vec[:, 1:2]).astype(BF)
        hidden = jnp.dot(expand[...], normed, preferred_element_type=F32) + bias[...]
        hidden = jax.nn.gelu(hidden, approximate=True).astype(BF)
        return jnp.dot(project[...], hidden, preferred_element_type=F32).astype(BF)

    air = unit(lanes(0, half_a), lanes(part, half_o), coup_a, vec_a, exp_a, eb_a, proj_a)
    sea = unit(lanes(half_a, half_o), lanes(part + half_o, half_a), coup_o, vec_o, exp_o, eb_o, proj_o)
    for y in range(rows):
        at = slice(y * 128, (y + 1) * 128)
        for side in range(2):
            out_ref[side, y, :half_a, :] = air[side * half_a : (side + 1) * half_a, at]
            out_ref[side, y, half_a:part, :] = sea[side * half_o : (side + 1) * half_o, at]


def finish_kernel(bounds, update_ref, atm_ref, sea_ref, atm_out, sea_out):
    for field, out, (low, high) in zip((atm_ref, sea_ref), (atm_out, sea_out), bounds):
        update = jnp.swapaxes(update_ref[:, low:high, :], 0, 1)
        out[...] = (field[...].astype(F32) + update.astype(F32)).astype(BF)


def slots_of(heading):
    lanes = heading[:, 0]
    n = lanes.shape[0]
    i = jnp.arange(n, dtype=jnp.int32)
    before = (lanes[:, None] == lanes[None, :]) & (i[None, :] < i[:, None])
    return lanes * SLOTS + jnp.sum(before.astype(jnp.int32), axis=1)


def local(
    atm, sea, atm_kernel, atm_coupling, atm_gain, atm_shift, atm_expand, atm_expand_bias, atm_project,
    sea_kernel, sea_coupling, sea_gain, sea_shift, sea_expand, sea_expand_bias, sea_project,
    flux_source, flux_target, flux_weight, flux_heading, sst_source, sst_target, sst_weight, sst_heading,
):
    n_tiles, n_rows = lax.axis_size("tiles"), lax.axis_size("rows")
    band = lax.axis_index("tiles")
    last = n_tiles - 1
    half_a, half_o = atm.shape[0], sea.shape[0]
    part = half_a + half_o
    height, width = atm.shape[1], atm.shape[2]
    blocks = flux_source.shape[0]
    bounds = ((0, half_a), (half_a, part))
    params = functools.partial(pltpu.CompilerParams, vmem_limit_bytes=VMEM_LIMIT)
    vmem = pl.BlockSpec(memory_space=pltpu.VMEM)
    smem = pl.BlockSpec(memory_space=pltpu.SMEM)

    slots = jnp.stack([slots_of(flux_heading), slots_of(sst_heading)])
    source = jnp.stack([flux_source, sst_source])
    target = jnp.stack([flux_target, sst_target])
    weight = jnp.stack([flux_weight, sst_weight])

    def paired(a):
        return a.astype(F32).reshape(2, blocks // 2, 1, 2 * 128)

    meta = jnp.stack([target // LANES, target % LANES], axis=1).astype(F32)[:, :, :, None, :]
    packed, state = pl.pallas_call(
        functools.partial(pack_kernel, bounds),
        out_shape=[
            jax.ShapeDtypeStruct((9, SLOTS + 1, 128, 128), BF),
            jax.ShapeDtypeStruct((height, part, 128), BF),
        ],
        in_specs=[smem] + [vmem] * 6,
        out_specs=[vmem, vmem],
        compiler_params=params(),
        name="pack",
    )(slots, atm, sea, paired(source % LANES), paired(source // LANES), paired(weight), meta)

    got = pl.pallas_call(
        functools.partial(send_kernel, n_tiles, n_rows),
        out_shape=jax.ShapeDtypeStruct((10, SLOTS + 1, 128, 128), BF),
        in_specs=[pl.BlockSpec(memory_space=pl.ANY)],
        out_specs=pl.BlockSpec(memory_space=pl.ANY),
        scratch_shapes=[
            pltpu.SemaphoreType.DMA((9,)),
            pltpu.SemaphoreType.DMA((9,)),
            pltpu.SemaphoreType.DMA,
        ],
        compiler_params=params(collective_id=0, has_side_effects=True),
        name="send",
    )(packed)

    def across(side):
        perm = [(s, n_rows - 1 - (s + side) % n_rows) for s in range(n_rows)]
        row = state[height - 1]
        if all(a == b for a, b in perm):
            return row
        return lax.ppermute(row, "rows", perm)

    taps = jnp.concatenate([atm_kernel, sea_kernel], axis=0).reshape(part, 9).T[:, :, None]
    taps = jnp.broadcast_to(taps, (9, part, 128))

    flags = jnp.stack([band == 0, band == last]).astype(jnp.int32)
    mixed_in = pl.pallas_call(
        functools.partial(land_kernel, bounds, (part + half_o, part)),
        out_shape=jax.ShapeDtypeStruct((height, 2 * part, 128), BF),
        in_specs=[smem] + [vmem] * 4,
        out_specs=vmem,
        scratch_shapes=[
            pltpu.VMEM((height // 2 * half_a, LANES), F32),
            pltpu.SMEM((2, 10 * SLOTS), jnp.int32),
        ],
        compiler_params=params(),
        name="land",
    )(flags, got.reshape(10 * (SLOTS + 1), 128, 128), state, jnp.stack([across(-1), across(1)]), taps)

    full = lax.all_to_all(mixed_in.reshape(2, height // 2, 2 * part, 128), "comp", split_axis=0, concat_axis=0)
    ca, co = 2 * half_a, 2 * half_o
    rows = 4

    def whole(a):
        return pl.BlockSpec(a.shape, lambda i: (0,) * a.ndim)

    weights = [
        atm_coupling, jnp.stack([atm_gain, atm_shift], axis=1), atm_expand, atm_expand_bias[:, None], atm_project,
        sea_coupling, jnp.stack([sea_gain, sea_shift], axis=1), sea_expand, sea_expand_bias[:, None], sea_project,
    ]
    update = pl.pallas_call(
        functools.partial(mix_kernel, ca, co),
        grid=(height // 2 // rows,),
        out_shape=jax.ShapeDtypeStruct((2, height // 2, part, 128), BF),
        in_specs=[pl.BlockSpec((2, rows, 2 * part, 128), lambda i: (0, i, 0, 0))] + [whole(a) for a in weights],
        out_specs=pl.BlockSpec((2, rows, part, 128), lambda i: (0, i, 0, 0)),
        compiler_params=params(),
        name="mix",
    )(full, *weights)
    update = lax.all_to_all(update, "comp", split_axis=0, concat_axis=0).reshape(height, part, 128)

    def band_of(chans):
        return pl.BlockSpec((chans, 16, 128), lambda i: (0, i, 0))

    return tuple(
        pl.pallas_call(
            functools.partial(finish_kernel, bounds),
            grid=(height // 16,),
            out_shape=[jax.ShapeDtypeStruct(atm.shape, BF), jax.ShapeDtypeStruct(sea.shape, BF)],
            in_specs=[pl.BlockSpec((16, part, 128), lambda i: (i, 0, 0)), band_of(half_a), band_of(half_o)],
            out_specs=[band_of(half_a), band_of(half_o)],
            compiler_params=params(),
            name="finish",
        )(update, atm, sea)
    )


def solution(mesh):
    grid = P(("groups", "comp"), "tiles", "rows")
    lists = P(("tiles", "rows"), None)
    taps = P("comp", None, None)
    placed = (grid, grid, taps) + (P(),) * 6 + (taps,) + (P(),) * 6 + (lists,) * 8
    return jax.shard_map(local, mesh=mesh, in_specs=placed, out_specs=(grid, grid), check_vma=False)
```

```python
import functools

import jax
import jax.numpy as jnp
from jax import lax
from jax.experimental import pallas as pl
from jax.experimental.pallas import tpu as pltpu
from jax.sharding import PartitionSpec as P

SLOTS = 16
LEVELS = (8, 10, 12, 16)
META = 112
LANES = 256
GROUP = 8
VMEM_LIMIT = 56 * 1024 * 1024
BF = jnp.bfloat16
F32 = jnp.float32
MESH = pl.DeviceIdType.MESH


def pack_kernel(bounds, slots_ref, atm_ref, sea_ref, pos_ref, high_ref, weight_ref, meta_ref, out_ref, state_ref):
    height = state_ref.shape[0]
    chans_all = state_ref.shape[1]
    pairs = height // 2
    for field, (low, high) in zip((atm_ref, sea_ref), bounds):
        for y in range(0, height, 16):
            state_ref[y : y + 16, low:high, :] = jnp.swapaxes(field[:, y : y + 16, :], 0, 1)

    def clear(i, _):
        out_ref[i // SLOTS, lax.rem(i, SLOTS) + 1, META:, :] = jnp.full((16, 128), -1, BF)
        return 0

    lax.fori_loop(0, 9 * SLOTS, clear, 0)

    row_at = lax.broadcasted_iota(jnp.int32, (128, LANES), 0)
    lane_at = lax.broadcasted_iota(jnp.int32, (128, LANES), 1)

    def column_of(y, total):
        pick = ((row_at == 0) & (lane_at == y)) | ((row_at == 127) & (lane_at == y + 128))
        return total + jnp.dot(state_ref[y], pick.astype(F32).astype(BF), preferred_element_type=F32)

    columns = lax.fori_loop(0, height, column_of, jnp.zeros((chans_all, LANES), F32)).astype(BF)
    for k in range(9):
        if k // 3 == 0:
            out_ref[k, 0, :chans_all, :] = state_ref[0]
        elif k // 3 == 2:
            out_ref[k, 0, :chans_all, :] = state_ref[height - 1]
        elif k == 3:
            out_ref[k, 0, :chans_all, :] = columns[:, :128]
        elif k == 5:
            out_ref[k, 0, :chans_all, :] = columns[:, 128:]

    column = lax.broadcasted_iota(jnp.int32, (LANES, LANES), 0).astype(F32).astype(BF)
    row16 = lax.broadcasted_iota(jnp.int32, (16, 128), 0)

    def step(j, _):
        for f, (low, high) in enumerate(bounds):
            chans = high - low
            hit = jnp.broadcast_to(pos_ref[f, j], (LANES, LANES)).astype(BF) == column
            onehot = jnp.where(hit, jnp.ones((), BF), jnp.zeros((), BF))
            wanted = jnp.broadcast_to(high_ref[f, j], (8, LANES))
            total = jnp.zeros((chans // 8, 8, LANES), F32)
            for first in range(0, pairs, GROUP):
                lhs = jnp.concatenate(
                    [
                        jnp.concatenate(
                            [state_ref[2 * q, low:high, :], state_ref[2 * q + 1, low:high, :]], axis=1
                        )
                        for q in range(first, first + GROUP)
                    ],
                    axis=0,
                )
                part = jnp.dot(lhs, onehot, preferred_element_type=F32)
                for q in range(GROUP):
                    piece = part[q * chans : (q + 1) * chans].reshape(total.shape)
                    total = jnp.where((wanted == float(first + q))[None], piece, total)
            values = (total.reshape(chans, LANES) * weight_ref[f, j]).astype(BF)
            for half in range(2):
                block = 2 * j + half
                slot = slots_ref[f, block]
                k, s = slot // SLOTS, lax.rem(slot, SLOTS) + 1
                out_ref[k, s, low:high, :] = values[:, half * 128 : (half + 1) * 128]
                old = out_ref[k, s, META:, :].astype(F32)
                for item in range(2):
                    place = jnp.broadcast_to(meta_ref[f, item, block], (16, 128))
                    old = jnp.where(row16 == 2 * f + item, place, old)
                out_ref[k, s, META:, :] = old.astype(BF)
        return 0

    lax.fori_loop(0, slots_ref.shape[1] // 2, step, 0)


def send_kernel(n_tiles, n_rows, cap, packed_ref, got_ref, send_sem, recv_sem, local_sem):
    band = lax.axis_index("tiles")
    strip = lax.axis_index("rows")
    last = n_tiles - 1
    barrier = pltpu.get_barrier_semaphore()
    routes = []
    for k in (0, 2, 6, 8, 3, 5, 1, 7):
        lift, side = k // 3 - 1, k % 3 - 1
        to = {"tiles": band + lift, "rows": lax.rem(strip + side + n_rows, n_rows)}
        sends = (band + lift >= 0) & (band + lift <= last)
        receives = (band - lift >= 0) & (band - lift <= last)
        routes.append((k, k, to, sends, receives))
    routes.append((7, 9, {"rows": n_rows - 1 - strip}, band == last, band == last))

    peers = []
    for lift in (-1, 0, 1):
        for side in (0, 1) if n_rows == 2 else (-1, 0, 1):
            if (lift, side) != (0, 0):
                to = {"tiles": band + lift, "rows": lax.rem(strip + side + n_rows, n_rows)}
                peers.append((to, (band + lift >= 0) & (band + lift <= last)))
    if n_rows > 2:
        mirror = n_rows - 1 - strip
        beside = (mirror == lax.rem(strip + 1, n_rows)) | (mirror == lax.rem(strip + n_rows - 1, n_rows))
        peers.append(({"rows": mirror}, (band == last) & jnp.logical_not(beside)))
    for to, there in peers:

        @pl.when(there)
        def _():
            pl.semaphore_signal(barrier, inc=1, device_id=to, device_id_type=MESH)

    pl.semaphore_wait(barrier, sum(there.astype(jnp.int32) for _, there in peers))

    def copy(i):
        src, dst, to, _, _ = routes[i]
        return pltpu.make_async_remote_copy(
            src_ref=packed_ref.at[src, pl.ds(0, cap + 1)],
            dst_ref=got_ref.at[dst, pl.ds(0, cap + 1)],
            send_sem=send_sem.at[i],
            recv_sem=recv_sem.at[i],
            device_id=to,
            device_id_type=MESH,
        )

    for i, route in enumerate(routes):

        @pl.when(route[3])
        def _():
            copy(i).start()

    own = pltpu.make_async_copy(packed_ref.at[4], got_ref.at[4], local_sem)
    own.start()
    own.wait()
    for i, route in enumerate(routes):

        @pl.when(route[3])
        def _():
            copy(i).wait_send()

        @pl.when(route[4])
        def _():
            copy(i).wait_recv()


def land_kernel(bounds, outs, flags_ref, got_ref, state_ref, across_ref, taps_ref, out_ref, acc_ref, order_ref):
    height = state_ref.shape[0]
    chans = state_ref.shape[1]
    stride = SLOTS + 1
    first_band, last_band = flags_ref[0] == 1, flags_ref[1] == 1
    row_of = lax.broadcasted_iota(jnp.int32, (256, 128), 0)
    lane_of = lax.broadcasted_iota(jnp.int32, (256, 128), 1)
    lane = lax.broadcasted_iota(jnp.int32, (chans, 128), 1)
    is_air = lax.broadcasted_iota(jnp.int32, (chans, 128), 0) < bounds[0][1]

    def edge(k):
        return got_ref[k * stride, :chans, :]

    cols = jnp.concatenate([edge(5), edge(3)], axis=1)
    wide = lax.broadcasted_iota(jnp.int32, (chans, 256), 1) % 128
    cols = jnp.where(wide < height, cols.astype(F32), 0.0).astype(BF)

    def spread(row, left, right):
        return [
            taps_ref[3 * r] * left + taps_ref[3 * r + 1] * row + taps_ref[3 * r + 2] * right
            for r in range(3)
        ]

    def taps(i, row):
        y = i - 1
        pick = ((row_of == y) & (lane_of == 0)) | ((row_of == y + 128) & (lane_of == 127))
        ends = jnp.dot(cols, pick.astype(F32).astype(BF), preferred_element_type=F32)
        row = row.astype(F32)
        left = jnp.where(lane == 0, ends, pltpu.roll(row, 1, 1))
        right = jnp.where(lane == 127, ends, pltpu.roll(row, 127, 1))
        return spread(row, left, right)

    def beyond(row, west, east):
        left = jnp.where(lane == 0, west, pltpu.roll(row, 1, 1))
        right = jnp.where(lane == 127, east, pltpu.roll(row, 127, 1))
        return row, left, right

    def row_from(middle, west, east):
        return beyond(
            edge(middle).astype(F32),
            pltpu.roll(edge(west).astype(F32), 1, 1),
            pltpu.roll(edge(east).astype(F32), 127, 1),
        )

    south = [jnp.where(first_band, 0.0, part) for part in row_from(7, 8, 6)]
    flip_row = lax.broadcasted_iota(jnp.int32, (128, 128), 0)
    flip_lane = lax.broadcasted_iota(jnp.int32, (128, 128), 1)
    flip = (flip_row + flip_lane == 127).astype(F32).astype(BF)
    fold = jnp.where(last_band, edge(9).astype(F32), 0.0).astype(BF)
    fold = jnp.dot(fold, flip, preferred_element_type=F32)
    folded = beyond(fold, across_ref[0].astype(F32), across_ref[1].astype(F32))
    north = [
        jnp.where(last_band, jnp.where(is_air, 0.0, over), part)
        for over, part in zip(folded, row_from(1, 2, 0))
    ]

    def put(y, value):
        value = value.astype(BF)
        out_ref[y, 0:chans, :] = value

    h0 = spread(*south)
    h1 = taps(1, state_ref[0])

    def conv(i, carry):
        older, newer = carry
        h = taps(i, state_ref[i - 1])
        put(i - 2, older + h[2])
        return newer + h[1], h[0]

    older, newer = lax.fori_loop(2, height + 1, conv, (h0[0] + h1[1], h1[0]))
    h = spread(*north)
    put(height - 1, older + h[2])

    column = lax.broadcasted_iota(jnp.int32, (LANES, GROUP * 128), 0).astype(F32).astype(BF)
    pairs = height // 2
    place_row = lax.broadcasted_iota(jnp.int32, (16, 128), 0)
    place_lane = lax.broadcasted_iota(jnp.int32, (16, 128), 1)
    slot_at = lax.broadcasted_iota(jnp.int32, (SLOTS, 16, 128), 0)
    counts = [jnp.int32(0), jnp.int32(0)]
    for k in range(10):
        places = got_ref[k * stride + 1 : (k + 1) * stride, META:, :].astype(F32)
        filled = jnp.sum(((places >= 0) & (slot_at < (SLOTS if k == 4 else flags_ref[2]))).astype(F32), axis=0)
        usable = True if 3 <= k < 6 else jnp.logical_not(last_band) if k < 3 else jnp.logical_not(first_band) if k < 9 else last_band
        for f in range(2):
            there = (place_row == 2 * f) & (place_lane == 0)
            count = jnp.sum(jnp.where(there, filled, 0.0)).astype(jnp.int32)
            count = jnp.where(usable, count, 0)
            base = counts[f]

            def note(i, _):
                order_ref[f, base + i] = k * stride + 1 + i
                return 0

            lax.fori_loop(0, count, note, 0)
            counts[f] = base + count
    for f, (low, high) in enumerate(bounds):
        width = high - low
        count = counts[f]
        acc_ref[...] = jnp.zeros_like(acc_ref)

        def step(j, _):
            vals, high_of, low_of = [], [], []
            for b in range(GROUP):
                at = order_ref[f, jnp.minimum(j * GROUP + b, count - 1)]
                vals.append(got_ref[at, low:high, :])
                meta = got_ref[at, META:, :].astype(F32)
                live = j * GROUP + b < count
                high_of.append(jnp.where(live, meta[2 * f : 2 * f + 1], -1.0))
                low_of.append(jnp.where(live, meta[2 * f + 1 : 2 * f + 2], -1.0))
            vals = jnp.concatenate(vals, axis=1)
            high_of = jnp.concatenate(high_of, axis=1)
            low_of = jnp.concatenate(low_of, axis=1)
            hit = jnp.broadcast_to(low_of, (LANES, GROUP * 128)).astype(BF) == column
            onehot = jnp.where(hit, jnp.ones((), BF), jnp.zeros((), BF))
            wanted = jnp.broadcast_to(high_of, (width, GROUP * 128)).astype(BF)
            for first in range(0, pairs, 8):
                lhs = jnp.concatenate(
                    [
                        jnp.where(wanted == jnp.asarray(first + q, BF), vals, jnp.zeros((), BF))
                        for q in range(8)
                    ],
                    axis=0,
                )
                acc_ref[first * width : (first + 8) * width, :] += lax.dot_general(
                    lhs, onehot, (((1,), (1,)), ((), ())), preferred_element_type=F32
                )
            return 0

        lax.fori_loop(0, (count + GROUP - 1) // GROUP, step, 0)
        begin = outs[f]
        for q in range(pairs):
            piece = acc_ref[q * width : (q + 1) * width, :].astype(BF)
            out_ref[2 * q, begin : begin + width, :] = piece[:, :128]
            out_ref[2 * q + 1, begin : begin + width, :] = piece[:, 128:]


def mix_kernel(ca, co, in_ref, coup_a, vec_a, exp_a, eb_a, proj_a, coup_o, vec_o, exp_o, eb_o, proj_o, out_ref):
    rows = in_ref.shape[1]
    half_a, half_o = ca // 2, co // 2
    part = half_a + half_o

    def lanes(low, size):
        return jnp.concatenate(
            [
                jnp.concatenate([in_ref[0, y, low : low + size, :], in_ref[1, y, low : low + size, :]], axis=0)
                for y in range(rows)
            ],
            axis=1,
        )

    def unit(conv, coupled, coup, vec, expand, bias, project):
        mixed = conv.astype(F32) + jnp.dot(coup[...], coupled, preferred_element_type=F32)
        mean = jnp.mean(mixed, axis=0, keepdims=True)
        centred = mixed - mean
        var = jnp.mean(centred * centred, axis=0, keepdims=True)
        normed = (centred * lax.rsqrt(var + 1e-6) * vec[:, 0:1] + vec[:, 1:2]).astype(BF)
        hidden = jnp.dot(expand[...], normed, preferred_element_type=F32) + bias[...]
        hidden = jax.nn.gelu(hidden, approximate=True).astype(BF)
        return jnp.dot(project[...], hidden, preferred_element_type=F32).astype(BF)

    air = unit(lanes(0, half_a), lanes(part, half_o), coup_a, vec_a, exp_a, eb_a, proj_a)
    sea = unit(lanes(half_a, half_o), lanes(part + half_o, half_a), coup_o, vec_o, exp_o, eb_o, proj_o)
    for y in range(rows):
        at = slice(y * 128, (y + 1) * 128)
        for side in range(2):
            out_ref[side, y, :half_a, :] = air[side * half_a : (side + 1) * half_a, at]
            out_ref[side, y, half_a:part, :] = sea[side * half_o : (side + 1) * half_o, at]


def finish_kernel(bounds, update_ref, atm_ref, sea_ref, atm_out, sea_out):
    for field, out, (low, high) in zip((atm_ref, sea_ref), (atm_out, sea_out), bounds):
        update = jnp.swapaxes(update_ref[:, low:high, :], 0, 1)
        out[...] = (field[...].astype(F32) + update.astype(F32)).astype(BF)


def slots_of(heading):
    lanes = heading[:, 0]
    n = lanes.shape[0]
    i = jnp.arange(n, dtype=jnp.int32)
    before = (lanes[:, None] == lanes[None, :]) & (i[None, :] < i[:, None])
    within = jnp.sum(before.astype(jnp.int32), axis=1)
    return lanes * SLOTS + within, jnp.max(jnp.where(lanes == 4, 0, within + 1))


def local(
    atm, sea, atm_kernel, atm_coupling, atm_gain, atm_shift, atm_expand, atm_expand_bias, atm_project,
    sea_kernel, sea_coupling, sea_gain, sea_shift, sea_expand, sea_expand_bias, sea_project,
    flux_source, flux_target, flux_weight, flux_heading, sst_source, sst_target, sst_weight, sst_heading,
):
    n_tiles, n_rows = lax.axis_size("tiles"), lax.axis_size("rows")
    band = lax.axis_index("tiles")
    last = n_tiles - 1
    half_a, half_o = atm.shape[0], sea.shape[0]
    part = half_a + half_o
    height, width = atm.shape[1], atm.shape[2]
    blocks = flux_source.shape[0]
    bounds = ((0, half_a), (half_a, part))
    params = functools.partial(pltpu.CompilerParams, vmem_limit_bytes=VMEM_LIMIT)
    vmem = pl.BlockSpec(memory_space=pltpu.VMEM)
    smem = pl.BlockSpec(memory_space=pltpu.SMEM)

    flux_slots, flux_most = slots_of(flux_heading)
    sst_slots, sst_most = slots_of(sst_heading)
    slots = jnp.stack([flux_slots, sst_slots])
    most = lax.pmax(jnp.maximum(flux_most, sst_most), ("groups", "tiles", "rows", "comp"))
    level = sum((most > cap).astype(jnp.int32) for cap in LEVELS[:-1])
    source = jnp.stack([flux_source, sst_source])
    target = jnp.stack([flux_target, sst_target])
    weight = jnp.stack([flux_weight, sst_weight])

    def paired(a):
        return a.astype(F32).reshape(2, blocks // 2, 1, 2 * 128)

    meta = jnp.stack([target // LANES, target % LANES], axis=1).astype(F32)[:, :, :, None, :]
    packed, state = pl.pallas_call(
        functools.partial(pack_kernel, bounds),
        out_shape=[
            jax.ShapeDtypeStruct((9, SLOTS + 1, 128, 128), BF),
            jax.ShapeDtypeStruct((height, part, 128), BF),
        ],
        in_specs=[smem] + [vmem] * 6,
        out_specs=[vmem, vmem],
        compiler_params=params(),
        name="pack",
    )(slots, atm, sea, paired(source % LANES), paired(source // LANES), paired(weight), meta)

    def send(index, cap):
        return pl.pallas_call(
            functools.partial(send_kernel, n_tiles, n_rows, cap),
            out_shape=jax.ShapeDtypeStruct((10, SLOTS + 1, 128, 128), BF),
            in_specs=[pl.BlockSpec(memory_space=pl.ANY)],
            out_specs=pl.BlockSpec(memory_space=pl.ANY),
            scratch_shapes=[
                pltpu.SemaphoreType.DMA((9,)),
                pltpu.SemaphoreType.DMA((9,)),
                pltpu.SemaphoreType.DMA,
            ],
            compiler_params=params(collective_id=index, has_side_effects=True),
            name=f"send{cap}",
        )

    got = lax.switch(level, [send(index, cap) for index, cap in enumerate(LEVELS)], packed)

    def across(side):
        perm = [(s, n_rows - 1 - (s + side) % n_rows) for s in range(n_rows)]
        row = state[height - 1]
        if all(a == b for a, b in perm):
            return row
        return lax.ppermute(row, "rows", perm)

    taps = jnp.concatenate([atm_kernel, sea_kernel], axis=0).reshape(part, 9).T[:, :, None]
    taps = jnp.broadcast_to(taps, (9, part, 128))

    cap = sum(jnp.where(level == index, cap, 0) for index, cap in enumerate(LEVELS))
    flags = jnp.stack([(band == 0).astype(jnp.int32), (band == last).astype(jnp.int32), cap])
    mixed_in = pl.pallas_call(
        functools.partial(land_kernel, bounds, (part + half_o, part)),
        out_shape=jax.ShapeDtypeStruct((height, 2 * part, 128), BF),
        in_specs=[smem] + [vmem] * 4,
        out_specs=vmem,
        scratch_shapes=[
            pltpu.VMEM((height // 2 * half_a, LANES), F32),
            pltpu.SMEM((2, 10 * SLOTS), jnp.int32),
        ],
        compiler_params=params(),
        name="land",
    )(flags, got.reshape(10 * (SLOTS + 1), 128, 128), state, jnp.stack([across(-1), across(1)]), taps)

    full = lax.all_to_all(mixed_in.reshape(2, height // 2, 2 * part, 128), "comp", split_axis=0, concat_axis=0)
    ca, co = 2 * half_a, 2 * half_o
    rows = 4

    def whole(a):
        return pl.BlockSpec(a.shape, lambda i: (0,) * a.ndim)

    weights = [
        atm_coupling, jnp.stack([atm_gain, atm_shift], axis=1), atm_expand, atm_expand_bias[:, None], atm_project,
        sea_coupling, jnp.stack([sea_gain, sea_shift], axis=1), sea_expand, sea_expand_bias[:, None], sea_project,
    ]
    update = pl.pallas_call(
        functools.partial(mix_kernel, ca, co),
        grid=(height // 2 // rows,),
        out_shape=jax.ShapeDtypeStruct((2, height // 2, part, 128), BF),
        in_specs=[pl.BlockSpec((2, rows, 2 * part, 128), lambda i: (0, i, 0, 0))] + [whole(a) for a in weights],
        out_specs=pl.BlockSpec((2, rows, part, 128), lambda i: (0, i, 0, 0)),
        compiler_params=params(),
        name="mix",
    )(full, *weights)
    update = lax.all_to_all(update, "comp", split_axis=0, concat_axis=0).reshape(height, part, 128)

    def band_of(chans):
        return pl.BlockSpec((chans, 16, 128), lambda i: (0, i, 0))

    return tuple(
        pl.pallas_call(
            functools.partial(finish_kernel, bounds),
            grid=(height // 16,),
            out_shape=[jax.ShapeDtypeStruct(atm.shape, BF), jax.ShapeDtypeStruct(sea.shape, BF)],
            in_specs=[pl.BlockSpec((16, part, 128), lambda i: (i, 0, 0)), band_of(half_a), band_of(half_o)],
            out_specs=[band_of(half_a), band_of(half_o)],
            compiler_params=params(),
            name="finish",
        )(update, atm, sea)
    )


def solution(mesh):
    grid = P(("groups", "comp"), "tiles", "rows")
    lists = P(("tiles", "rows"), None)
    taps = P("comp", None, None)
    placed = (grid, grid, taps) + (P(),) * 6 + (taps,) + (P(),) * 6 + (lists,) * 8
    return jax.shard_map(local, mesh=mesh, in_specs=placed, out_specs=(grid, grid), check_vma=False)
```

```python
import functools

import jax
import jax.numpy as jnp
from jax import lax
from jax.experimental import pallas as pl
from jax.experimental.pallas import tpu as pltpu
from jax.sharding import PartitionSpec as P

SLOTS = 16
LEVELS = (8, 10, 12, 16)
META = 112
LANES = 256
GROUP = 8
VMEM_LIMIT = 56 * 1024 * 1024
BF = jnp.bfloat16
F32 = jnp.float32
MESH = pl.DeviceIdType.MESH


def pack_kernel(bounds, slots_ref, atm_ref, sea_ref, pos_ref, high_ref, weight_ref, meta_ref, out_ref, state_ref):
    height = state_ref.shape[0]
    chans_all = state_ref.shape[1]
    pairs = height // 2
    for field, (low, high) in zip((atm_ref, sea_ref), bounds):
        for y in range(0, height, 16):
            state_ref[y : y + 16, low:high, :] = jnp.swapaxes(field[:, y : y + 16, :], 0, 1)

    def clear(i, _):
        out_ref[i // SLOTS, lax.rem(i, SLOTS) + 1, META:, :] = jnp.full((16, 128), -1, BF)
        return 0

    lax.fori_loop(0, 9 * SLOTS, clear, 0)

    row_at = lax.broadcasted_iota(jnp.int32, (128, LANES), 0)
    lane_at = lax.broadcasted_iota(jnp.int32, (128, LANES), 1)

    def column_of(y, total):
        pick = ((row_at == 0) & (lane_at == y)) | ((row_at == 127) & (lane_at == y + 128))
        return total + jnp.dot(state_ref[y], pick.astype(F32).astype(BF), preferred_element_type=F32)

    columns = lax.fori_loop(0, height, column_of, jnp.zeros((chans_all, LANES), F32)).astype(BF)
    for k in range(9):
        if k // 3 == 0:
            out_ref[k, 0, :chans_all, :] = state_ref[0]
        elif k // 3 == 2:
            out_ref[k, 0, :chans_all, :] = state_ref[height - 1]
        elif k == 3:
            out_ref[k, 0, :chans_all, :] = columns[:, :128]
        elif k == 5:
            out_ref[k, 0, :chans_all, :] = columns[:, 128:]

    column = lax.broadcasted_iota(jnp.int32, (LANES, LANES), 0).astype(F32).astype(BF)
    row16 = lax.broadcasted_iota(jnp.int32, (16, 128), 0)

    def step(j, _):
        for f, (low, high) in enumerate(bounds):
            chans = high - low
            hit = jnp.broadcast_to(pos_ref[f, j], (LANES, LANES)).astype(BF) == column
            onehot = jnp.where(hit, jnp.ones((), BF), jnp.zeros((), BF))
            wanted = jnp.broadcast_to(high_ref[f, j], (8, LANES))
            total = jnp.zeros((chans // 8, 8, LANES), F32)
            for first in range(0, pairs, GROUP):
                lhs = jnp.concatenate(
                    [
                        jnp.concatenate(
                            [state_ref[2 * q, low:high, :], state_ref[2 * q + 1, low:high, :]], axis=1
                        )
                        for q in range(first, first + GROUP)
                    ],
                    axis=0,
                )
                part = jnp.dot(lhs, onehot, preferred_element_type=F32)
                for q in range(GROUP):
                    piece = part[q * chans : (q + 1) * chans].reshape(total.shape)
                    total = jnp.where((wanted == float(first + q))[None], piece, total)
            values = (total.reshape(chans, LANES) * weight_ref[f, j]).astype(BF)
            for half in range(2):
                block = 2 * j + half
                slot = slots_ref[f, block]
                k, s = slot // SLOTS, lax.rem(slot, SLOTS) + 1
                out_ref[k, s, low:high, :] = values[:, half * 128 : (half + 1) * 128]
                old = out_ref[k, s, META:, :].astype(F32)
                for item in range(2):
                    place = jnp.broadcast_to(meta_ref[f, item, block], (16, 128))
                    old = jnp.where(row16 == 2 * f + item, place, old)
                out_ref[k, s, META:, :] = old.astype(BF)
        return 0

    lax.fori_loop(0, slots_ref.shape[1] // 2, step, 0)


def send_kernel(n_tiles, n_rows, cap, packed_ref, got_ref, send_sem, recv_sem, local_sem):
    band = lax.axis_index("tiles")
    strip = lax.axis_index("rows")
    last = n_tiles - 1
    barrier = pltpu.get_barrier_semaphore()
    routes = []
    for k in (0, 2, 6, 8, 3, 5, 1, 7):
        lift, side = k // 3 - 1, k % 3 - 1
        to = {"tiles": band + lift, "rows": lax.rem(strip + side + n_rows, n_rows)}
        sends = (band + lift >= 0) & (band + lift <= last)
        receives = (band - lift >= 0) & (band - lift <= last)
        routes.append((k, k, to, sends, receives))
    routes.append((7, 9, {"rows": n_rows - 1 - strip}, band == last, band == last))

    peers = []
    for lift in (-1, 0, 1):
        for side in (0, 1) if n_rows == 2 else (-1, 0, 1):
            if (lift, side) != (0, 0):
                to = {"tiles": band + lift, "rows": lax.rem(strip + side + n_rows, n_rows)}
                peers.append((to, (band + lift >= 0) & (band + lift <= last)))
    if n_rows > 2:
        mirror = n_rows - 1 - strip
        beside = (mirror == lax.rem(strip + 1, n_rows)) | (mirror == lax.rem(strip + n_rows - 1, n_rows))
        peers.append(({"rows": mirror}, (band == last) & jnp.logical_not(beside)))
    for to, there in peers:

        @pl.when(there)
        def _():
            pl.semaphore_signal(barrier, inc=1, device_id=to, device_id_type=MESH)

    pl.semaphore_wait(barrier, sum(there.astype(jnp.int32) for _, there in peers))

    def copy(i):
        src, dst, to, _, _ = routes[i]
        return pltpu.make_async_remote_copy(
            src_ref=packed_ref.at[src, pl.ds(0, cap + 1)],
            dst_ref=got_ref.at[dst, pl.ds(0, cap + 1)],
            send_sem=send_sem.at[i],
            recv_sem=recv_sem.at[i],
            device_id=to,
            device_id_type=MESH,
        )

    for i, route in enumerate(routes):

        @pl.when(route[3])
        def _():
            copy(i).start()

    own = pltpu.make_async_copy(packed_ref.at[4], got_ref.at[4], local_sem)
    own.start()
    own.wait()
    for i, route in enumerate(routes):

        @pl.when(route[3])
        def _():
            copy(i).wait_send()

        @pl.when(route[4])
        def _():
            copy(i).wait_recv()


def land_kernel(bounds, outs, flags_ref, got_ref, state_ref, across_ref, taps_ref, out_ref, acc_ref, order_ref):
    height = state_ref.shape[0]
    chans = state_ref.shape[1]
    stride = SLOTS + 1
    first_band, last_band = flags_ref[0] == 1, flags_ref[1] == 1
    row_of = lax.broadcasted_iota(jnp.int32, (256, 128), 0)
    lane_of = lax.broadcasted_iota(jnp.int32, (256, 128), 1)
    lane = lax.broadcasted_iota(jnp.int32, (chans, 128), 1)
    is_air = lax.broadcasted_iota(jnp.int32, (chans, 128), 0) < bounds[0][1]

    def edge(k):
        return got_ref[k * stride, :chans, :]

    cols = jnp.concatenate([edge(5), edge(3)], axis=1)
    wide = lax.broadcasted_iota(jnp.int32, (chans, 256), 1) % 128
    cols = jnp.where(wide < height, cols.astype(F32), 0.0).astype(BF)

    def spread(row, left, right):
        return [
            taps_ref[3 * r] * left + taps_ref[3 * r + 1] * row + taps_ref[3 * r + 2] * right
            for r in range(3)
        ]

    def taps(i, row):
        y = i - 1
        pick = ((row_of == y) & (lane_of == 0)) | ((row_of == y + 128) & (lane_of == 127))
        ends = jnp.dot(cols, pick.astype(F32).astype(BF), preferred_element_type=F32)
        row = row.astype(F32)
        left = jnp.where(lane == 0, ends, pltpu.roll(row, 1, 1))
        right = jnp.where(lane == 127, ends, pltpu.roll(row, 127, 1))
        return spread(row, left, right)

    def beyond(row, west, east):
        left = jnp.where(lane == 0, west, pltpu.roll(row, 1, 1))
        right = jnp.where(lane == 127, east, pltpu.roll(row, 127, 1))
        return row, left, right

    def row_from(middle, west, east):
        return beyond(
            edge(middle).astype(F32),
            pltpu.roll(edge(west).astype(F32), 1, 1),
            pltpu.roll(edge(east).astype(F32), 127, 1),
        )

    south = [jnp.where(first_band, 0.0, part) for part in row_from(7, 8, 6)]
    flip_row = lax.broadcasted_iota(jnp.int32, (128, 128), 0)
    flip_lane = lax.broadcasted_iota(jnp.int32, (128, 128), 1)
    flip = (flip_row + flip_lane == 127).astype(F32).astype(BF)
    fold = jnp.where(last_band, edge(9).astype(F32), 0.0).astype(BF)
    fold = jnp.dot(fold, flip, preferred_element_type=F32)
    folded = beyond(fold, across_ref[0].astype(F32), across_ref[1].astype(F32))
    north = [
        jnp.where(last_band, jnp.where(is_air, 0.0, over), part)
        for over, part in zip(folded, row_from(1, 2, 0))
    ]

    def put(y, value):
        value = value.astype(BF)
        out_ref[y, 0:chans, :] = value

    h0 = spread(*south)
    h1 = taps(1, state_ref[0])

    def conv(i, carry):
        older, newer = carry
        h = taps(i, state_ref[i - 1])
        put(i - 2, older + h[2])
        return newer + h[1], h[0]

    older, newer = lax.fori_loop(2, height + 1, conv, (h0[0] + h1[1], h1[0]))
    h = spread(*north)
    put(height - 1, older + h[2])

    column = lax.broadcasted_iota(jnp.int32, (LANES, GROUP * 128), 0).astype(F32).astype(BF)
    pairs = height // 2
    place_row = lax.broadcasted_iota(jnp.int32, (16, 128), 0)
    place_lane = lax.broadcasted_iota(jnp.int32, (16, 128), 1)
    slot_at = lax.broadcasted_iota(jnp.int32, (SLOTS, 16, 128), 0)
    counts = [jnp.int32(0), jnp.int32(0)]
    for k in range(10):
        places = got_ref[k * stride + 1 : (k + 1) * stride, META:, :].astype(F32)
        filled = jnp.sum(((places >= 0) & (slot_at < (SLOTS if k == 4 else flags_ref[2]))).astype(F32), axis=0)
        usable = True if 3 <= k < 6 else jnp.logical_not(last_band) if k < 3 else jnp.logical_not(first_band) if k < 9 else last_band
        for f in range(2):
            there = (place_row == 2 * f) & (place_lane == 0)
            count = jnp.sum(jnp.where(there, filled, 0.0)).astype(jnp.int32)
            count = jnp.where(usable, count, 0)
            base = counts[f]

            def note(i, _):
                order_ref[f, base + i] = k * stride + 1 + i
                return 0

            lax.fori_loop(0, count, note, 0)
            counts[f] = base + count
    for f, (low, high) in enumerate(bounds):
        width = high - low
        count = counts[f]
        acc_ref[...] = jnp.zeros_like(acc_ref)

        def step(j, _):
            vals, high_of, low_of = [], [], []
            for b in range(GROUP):
                at = order_ref[f, jnp.minimum(j * GROUP + b, count - 1)]
                vals.append(got_ref[at, low:high, :])
                meta = got_ref[at, META:, :].astype(F32)
                live = j * GROUP + b < count
                high_of.append(jnp.where(live, meta[2 * f : 2 * f + 1], -1.0))
                low_of.append(jnp.where(live, meta[2 * f + 1 : 2 * f + 2], -1.0))
            vals = jnp.concatenate(vals, axis=1)
            high_of = jnp.concatenate(high_of, axis=1)
            low_of = jnp.concatenate(low_of, axis=1)
            hit = jnp.broadcast_to(low_of, (LANES, GROUP * 128)).astype(BF) == column
            onehot = jnp.where(hit, jnp.ones((), BF), jnp.zeros((), BF))
            wanted = jnp.broadcast_to(high_of, (width, GROUP * 128)).astype(BF)
            for first in range(0, pairs, 8):
                lhs = jnp.concatenate(
                    [
                        jnp.where(wanted == jnp.asarray(first + q, BF), vals, jnp.zeros((), BF))
                        for q in range(8)
                    ],
                    axis=0,
                )
                acc_ref[first * width : (first + 8) * width, :] += lax.dot_general(
                    lhs, onehot, (((1,), (1,)), ((), ())), preferred_element_type=F32
                )
            return 0

        lax.fori_loop(0, (count + GROUP - 1) // GROUP, step, 0)
        begin = outs[f]
        for q in range(pairs):
            piece = acc_ref[q * width : (q + 1) * width, :].astype(BF)
            out_ref[2 * q, begin : begin + width, :] = piece[:, :128]
            out_ref[2 * q + 1, begin : begin + width, :] = piece[:, 128:]


def mix_kernel(ca, co, in_ref, coup_a, vec_a, exp_a, eb_a, proj_a, coup_o, vec_o, exp_o, eb_o, proj_o, out_ref):
    rows = in_ref.shape[1]
    half_a, half_o = ca // 2, co // 2
    part = half_a + half_o

    def lanes(low, size):
        return jnp.concatenate(
            [
                jnp.concatenate([in_ref[0, y, low : low + size, :], in_ref[1, y, low : low + size, :]], axis=0)
                for y in range(rows)
            ],
            axis=1,
        )

    def unit(conv, coupled, coup, vec, expand, bias, project):
        mixed = conv.astype(F32) + jnp.dot(coup[...], coupled, preferred_element_type=F32)
        mean = jnp.mean(mixed, axis=0, keepdims=True)
        centred = mixed - mean
        var = jnp.mean(centred * centred, axis=0, keepdims=True)
        normed = (centred * lax.rsqrt(var + 1e-6) * vec[:, 0:1] + vec[:, 1:2]).astype(BF)
        hidden = jnp.dot(expand[...], normed, preferred_element_type=F32) + bias[...]
        hidden = jax.nn.gelu(hidden, approximate=True).astype(BF)
        return jnp.dot(project[...], hidden, preferred_element_type=F32).astype(BF)

    air = unit(lanes(0, half_a), lanes(part, half_o), coup_a, vec_a, exp_a, eb_a, proj_a)
    sea = unit(lanes(half_a, half_o), lanes(part + half_o, half_a), coup_o, vec_o, exp_o, eb_o, proj_o)
    for y in range(rows):
        at = slice(y * 128, (y + 1) * 128)
        for side in range(2):
            out_ref[side, y, :half_a, :] = air[side * half_a : (side + 1) * half_a, at]
            out_ref[side, y, half_a:part, :] = sea[side * half_o : (side + 1) * half_o, at]


def finish_kernel(bounds, update_ref, atm_ref, sea_ref, atm_out, sea_out):
    for field, out, (low, high) in zip((atm_ref, sea_ref), (atm_out, sea_out), bounds):
        update = jnp.swapaxes(update_ref[:, low:high, :], 0, 1)
        out[...] = (field[...].astype(F32) + update.astype(F32)).astype(BF)


def slots_of(heading):
    lanes = heading[:, 0]
    n = lanes.shape[0]
    i = jnp.arange(n, dtype=jnp.int32)
    before = (lanes[:, None] == lanes[None, :]) & (i[None, :] < i[:, None])
    within = jnp.sum(before.astype(jnp.int32), axis=1)
    return lanes * SLOTS + within, jnp.max(jnp.where(lanes == 4, 0, within + 1))


def local(
    atm, sea, atm_kernel, atm_coupling, atm_gain, atm_shift, atm_expand, atm_expand_bias, atm_project,
    sea_kernel, sea_coupling, sea_gain, sea_shift, sea_expand, sea_expand_bias, sea_project,
    flux_source, flux_target, flux_weight, flux_heading, sst_source, sst_target, sst_weight, sst_heading,
):
    n_tiles, n_rows = lax.axis_size("tiles"), lax.axis_size("rows")
    band = lax.axis_index("tiles")
    last = n_tiles - 1
    half_a, half_o = atm.shape[0], sea.shape[0]
    part = half_a + half_o
    height, width = atm.shape[1], atm.shape[2]
    blocks = flux_source.shape[0]
    bounds = ((0, half_a), (half_a, part))
    params = functools.partial(pltpu.CompilerParams, vmem_limit_bytes=VMEM_LIMIT)
    vmem = pl.BlockSpec(memory_space=pltpu.VMEM)
    smem = pl.BlockSpec(memory_space=pltpu.SMEM)

    flux_slots, flux_most = slots_of(flux_heading)
    sst_slots, sst_most = slots_of(sst_heading)
    slots = jnp.stack([flux_slots, sst_slots])
    most = jnp.broadcast_to(jnp.maximum(flux_most, sst_most), (1, 128)).astype(jnp.int32)
    for axis, count in (("rows", n_rows), ("tiles", n_tiles)):
        shift = 1
        while shift < count:
            ring = [(i, (i + shift) % count) for i in range(count)]
            most = jnp.maximum(most, lax.ppermute(most, axis, ring))
            shift *= 2
    most = most[0, 0]
    level = sum((most > cap).astype(jnp.int32) for cap in LEVELS[:-1])
    source = jnp.stack([flux_source, sst_source])
    target = jnp.stack([flux_target, sst_target])
    weight = jnp.stack([flux_weight, sst_weight])

    def paired(a):
        return a.astype(F32).reshape(2, blocks // 2, 1, 2 * 128)

    meta = jnp.stack([target // LANES, target % LANES], axis=1).astype(F32)[:, :, :, None, :]
    packed, state = pl.pallas_call(
        functools.partial(pack_kernel, bounds),
        out_shape=[
            jax.ShapeDtypeStruct((9, SLOTS + 1, 128, 128), BF),
            jax.ShapeDtypeStruct((height, part, 128), BF),
        ],
        in_specs=[smem] + [vmem] * 6,
        out_specs=[vmem, vmem],
        compiler_params=params(),
        cost_estimate=pl.CostEstimate(flops=20_000_000_000, bytes_accessed=10_000_000, transcendentals=0),
        name="pack",
    )(slots, atm, sea, paired(source % LANES), paired(source // LANES), paired(weight), meta)

    def send(index, cap):
        return pl.pallas_call(
            functools.partial(send_kernel, n_tiles, n_rows, cap),
            out_shape=jax.ShapeDtypeStruct((10, SLOTS + 1, 128, 128), BF),
            in_specs=[pl.BlockSpec(memory_space=pl.ANY)],
            out_specs=pl.BlockSpec(memory_space=pl.ANY),
            scratch_shapes=[
                pltpu.SemaphoreType.DMA((9,)),
                pltpu.SemaphoreType.DMA((9,)),
                pltpu.SemaphoreType.DMA,
            ],
            compiler_params=params(collective_id=index, has_side_effects=True),
            name=f"send{cap}",
        )

    got = lax.switch(level, [send(index, cap) for index, cap in enumerate(LEVELS)], packed)

    def across(side):
        perm = [(s, n_rows - 1 - (s + side) % n_rows) for s in range(n_rows)]
        row = state[height - 1]
        if all(a == b for a, b in perm):
            return row
        return lax.ppermute(row, "rows", perm)

    taps = jnp.concatenate([atm_kernel, sea_kernel], axis=0).reshape(part, 9).T[:, :, None]
    taps = jnp.broadcast_to(taps, (9, part, 128))

    cap = sum(jnp.where(level == index, cap, 0) for index, cap in enumerate(LEVELS))
    flags = jnp.stack([(band == 0).astype(jnp.int32), (band == last).astype(jnp.int32), cap])
    mixed_in = pl.pallas_call(
        functools.partial(land_kernel, bounds, (part + half_o, part)),
        out_shape=jax.ShapeDtypeStruct((height, 2 * part, 128), BF),
        in_specs=[smem] + [vmem] * 4,
        out_specs=vmem,
        scratch_shapes=[
            pltpu.VMEM((height // 2 * half_a, LANES), F32),
            pltpu.SMEM((2, 10 * SLOTS), jnp.int32),
        ],
        compiler_params=params(),
        name="land",
    )(flags, got.reshape(10 * (SLOTS + 1), 128, 128), state, jnp.stack([across(-1), across(1)]), taps)

    full = lax.all_to_all(mixed_in.reshape(2, height // 2, 2 * part, 128), "comp", split_axis=0, concat_axis=0)
    ca, co = 2 * half_a, 2 * half_o
    rows = 4

    def whole(a):
        return pl.BlockSpec(a.shape, lambda i: (0,) * a.ndim)

    weights = [
        atm_coupling, jnp.stack([atm_gain, atm_shift], axis=1), atm_expand, atm_expand_bias[:, None], atm_project,
        sea_coupling, jnp.stack([sea_gain, sea_shift], axis=1), sea_expand, sea_expand_bias[:, None], sea_project,
    ]
    update = pl.pallas_call(
        functools.partial(mix_kernel, ca, co),
        grid=(height // 2 // rows,),
        out_shape=jax.ShapeDtypeStruct((2, height // 2, part, 128), BF),
        in_specs=[pl.BlockSpec((2, rows, 2 * part, 128), lambda i: (0, i, 0, 0))] + [whole(a) for a in weights],
        out_specs=pl.BlockSpec((2, rows, part, 128), lambda i: (0, i, 0, 0)),
        compiler_params=params(),
        name="mix",
    )(full, *weights)
    update = lax.all_to_all(update, "comp", split_axis=0, concat_axis=0).reshape(height, part, 128)

    def band_of(chans):
        return pl.BlockSpec((chans, 16, 128), lambda i: (0, i, 0))

    return tuple(
        pl.pallas_call(
            functools.partial(finish_kernel, bounds),
            grid=(height // 16,),
            out_shape=[jax.ShapeDtypeStruct(atm.shape, BF), jax.ShapeDtypeStruct(sea.shape, BF)],
            in_specs=[pl.BlockSpec((16, part, 128), lambda i: (i, 0, 0)), band_of(half_a), band_of(half_o)],
            out_specs=[band_of(half_a), band_of(half_o)],
            compiler_params=params(),
            name="finish",
        )(update, atm, sea)
    )


def solution(mesh):
    grid = P(("groups", "comp"), "tiles", "rows")
    lists = P(("tiles", "rows"), None)
    taps = P("comp", None, None)
    placed = (grid, grid, taps) + (P(),) * 6 + (taps,) + (P(),) * 6 + (lists,) * 8
    return jax.shard_map(local, mesh=mesh, in_specs=placed, out_specs=(grid, grid), check_vma=False)
```
